32 devices in a mesh: row: 4 (over z), col: 8 (over y, x, core).
Axes of the slice: x: 2, y: 2, z: 4, core: 2. Of those that a mesh axis runs over, the one named last changes fastest.
Arguments:
- contribution: float32 [1024, 6144], P('row', 'col'), may hold values from -6 to 6
- left_basis: bfloat16 [8, 8, 64, 1024], P(None, 'col', None, 'row'), may hold values from -6 to 6
- left_coef: bfloat16 [8, 8, 64, 1024], P(None, 'col', None, 'row'), may hold values from -0.75 to 0.75
- right_coef: bfloat16 [8, 4, 64, 2048], P(None, 'row', None, 'col'), may hold values from -0.75 to 0.75
- right_basis: bfloat16 [8, 4, 64, 6144], P(None, 'row', None, 'col'), may hold values from -6 to 6
- left_rank: int32 [8, 4], P(None, 'row'), may hold values from 8 to 64
- left_scale: float32 [8, 4], P(None, 'row'), may hold values from 0.08 to 0.8
- right_rank: int32 [8, 8], P(None, 'col'), may hold values from 8 to 64
- right_scale: float32 [8, 8], P(None, 'col'), may hold values from 0.08 to 0.8
- left_owner: int32 [8], replicated, may hold values from 0 to 7
- right_owner: int32 [8], replicated, may hold values from 0 to 3
Outputs:
- updated: float32 [1024, 6144], P('row', 'col')
The draws below stay inside these ranges and needn't reach their ends.
All inputs are finite; a program needn't handle non-finite values.
Results may differ from the reference program's by a relative error of at most 0.0003.
Values may be sent and summed in bfloat16 or wider, within the bound.
No kernel may reach another device: no remote copies, remote signals or barrier semaphores. Data moves between devices by JAX's collectives and lax.ppermute only.
A program may use at most 64 MiB of HBM per device.

```python
import math
import jax
import jax.numpy as jnp
from jax import lax

PANEL = 256
RMAX = 64
PANELS = 8
ROW_DEV = 256
COL_DEV = 768
ROW_GROUPS = 4
COL_GROUPS = 8
ROWS = 1024
COLS = 6144
N_ROW = 4
N_COL = 8


def place_ends(drawn, key, low, high):
    index_at = [jax.random.randint(jax.random.fold_in(key, axis), (), 0, length) for axis, length in enumerate(drawn.shape)]
    main_axis = drawn.shape.index(max(drawn.shape))
    next_to = index_at[:main_axis] + [(index_at[main_axis] + 1) % drawn.shape[main_axis]] + index_at[main_axis + 1:]
    return drawn.at[tuple(index_at)].set(low).at[tuple(next_to)].set(high)


def block_scale(stream_key, shape, cuts, least, largest):
    def one(axis_at, blocks):
        steps = jax.random.uniform(jax.random.fold_in(jax.random.fold_in(stream_key, 6), axis_at), (blocks,), jnp.float32, least / len(cuts), largest / len(cuts))
        return jnp.repeat(jnp.exp(steps), shape[axis_at] // blocks).reshape((-1,) + (1,) * (len(shape) - axis_at - 1))

    gain = one(*cuts[0])
    for cut in cuts[1:]:
        gain = gain * one(*cut)
    return gain


def gaussian(stream_key, dims, scale, most, pieces=(), dtype=jnp.bfloat16):
    factor_of = block_scale(stream_key, dims, pieces, -0.22, 0.18) if pieces else 1.0
    result = jax.random.normal(stream_key, dims, jnp.float32) * scale * factor_of
    return jnp.minimum(jnp.maximum(result, -most), most).astype(dtype)


def setup_inputs(seed: int = 0) -> dict:
    streams_of = jax.random.split(jax.random.key(seed), 12)
    return {
        "contribution": gaussian(streams_of[0], (ROWS, COLS), 1.0, 6.0, ((0, 4), (1, 8)), jnp.float32),
        "left_basis": gaussian(streams_of[1], (PANELS, COL_GROUPS, RMAX, ROWS), 1.0, 6.0, ((1, 8), (3, 4))),
        "left_coef": gaussian(streams_of[2], (PANELS, COL_GROUPS, RMAX, ROW_GROUPS * PANEL), RMAX ** -0.5, 0.75, ((1, 8), (3, 4))),
        "right_coef": gaussian(streams_of[3], (PANELS, ROW_GROUPS, RMAX, COL_GROUPS * PANEL), RMAX ** -0.5, 0.75, ((1, 4), (3, 8))),
        "right_basis": gaussian(streams_of[4], (PANELS, ROW_GROUPS, RMAX, COLS), 1.0, 6.0, ((1, 4), (3, 8))),
        "left_rank": place_ends(jax.random.randint(streams_of[5], (PANELS, ROW_GROUPS), 8, RMAX + 1), jax.random.fold_in(streams_of[5], 1), 8, RMAX).astype(jnp.int32),
        "left_scale": jnp.clip(jnp.exp(math.log(0.8) - 2.3025851 * jax.random.uniform(streams_of[6], (PANELS, ROW_GROUPS), jnp.float32) ** block_scale(streams_of[6], (PANELS, ROW_GROUPS), ((1, 4),), -0.2, 0.2)), 0.08, 0.8),
        "right_rank": place_ends(jax.random.randint(streams_of[7], (PANELS, COL_GROUPS), 8, RMAX + 1), jax.random.fold_in(streams_of[7], 1), 8, RMAX).astype(jnp.int32),
        "right_scale": jnp.clip(jnp.exp(math.log(0.8) - 2.3025851 * jax.random.uniform(streams_of[8], (PANELS, COL_GROUPS), jnp.float32) ** block_scale(streams_of[8], (PANELS, COL_GROUPS), ((1, 8),), -0.2, 0.2)), 0.08, 0.8),
        "left_owner": place_ends(jax.random.randint(streams_of[9], (PANELS,), 0, COL_GROUPS), jax.random.fold_in(streams_of[9], 1), 0, COL_GROUPS - 1).astype(jnp.int32),
        "right_owner": place_ends(jax.random.randint(streams_of[10], (PANELS,), 0, ROW_GROUPS), jax.random.fold_in(streams_of[10], 1), 0, ROW_GROUPS - 1).astype(jnp.int32),
    }


def reference(contribution, left_basis, left_coef, right_coef, right_basis, left_rank, left_scale, right_rank, right_scale, left_owner, right_owner):
    hp = lax.Precision.HIGHEST
    slots = jnp.arange(RMAX)
    total = jnp.zeros((N_ROW, ROW_DEV, N_COL, COL_DEV), jnp.float32)
    for panel in range(PANELS):
        lo = left_owner[panel]
        ro = right_owner[panel]
        xb = left_basis[panel][lo].astype(jnp.float32).reshape(RMAX, N_ROW, ROW_DEV)
        yb = left_coef[panel][lo].astype(jnp.float32).reshape(RMAX, N_ROW, PANEL)
        zb = right_coef[panel][ro].astype(jnp.float32).reshape(RMAX, N_COL, PANEL)
        wb = right_basis[panel][ro].astype(jnp.float32).reshape(RMAX, N_COL, COL_DEV)
        lweight = jnp.where(slots[None, :] < left_rank[panel][:, None], left_scale[panel][:, None], jnp.float32(0.0))
        rweight = jnp.where(slots[None, :] < right_rank[panel][:, None], right_scale[panel][:, None], jnp.float32(0.0))
        xb = xb * lweight.T[:, :, None]
        zb = zb * rweight.T[:, :, None]
        core = jnp.einsum('kip,ljp->ijkl', yb, zb, precision=hp)
        middle = jnp.einsum('ijkl,ljc->ijkc', core, wb, precision=hp)
        total = total + jnp.einsum('kir,ijkc->irjc', xb, middle, precision=hp)
    return contribution - total.reshape(N_ROW * ROW_DEV, N_COL * COL_DEV)
```

```python
import functools

import jax
import jax.numpy as jnp
from jax import lax
from jax.experimental import pallas as pl
from jax.experimental.pallas import tpu as pltpu
from jax.sharding import PartitionSpec as P

PLANS = ((2, 2), (3, 2), (4, 2), (2, 3), (3, 3), (5, 2), (4, 4))
INWARD = ((0, 1), (3, 2))
OUTWARD = ((1, 0), (2, 3))
MIDDLE = ((1, 2), (2, 1))


def flip(x, axis, size, bit):
    return lax.ppermute(x, axis, [(i, i ^ bit) for i in range(size)])


def same_bit(owner, me, bit):
    return ((owner & bit) == (me & bit))[:, None, None]


def spread_left(basis, coef, owner, size):
    me = lax.axis_index("col")
    half = basis.shape[0] // 2
    keep = same_bit(owner, me, 1)
    first = (me & 1) * half

    def mine(x):
        return lax.dynamic_slice_in_dim(jnp.where(keep, x, flip(x, "col", size, 1)), first, half)

    held = jnp.concatenate([mine(basis), mine(coef)], axis=2)
    owner = lax.dynamic_slice_in_dim(owner, first, half)
    bit = 2
    while bit < size:
        held = jnp.where(same_bit(owner, me, bit), held, flip(held, "col", size, bit))
        bit *= 2
    return held, flip(held, "col", size, 1)


def spread_right(x, owner, size):
    me = lax.axis_index("row")
    bit = 1
    while bit < size:
        x = jnp.where(same_bit(owner, me, bit), x, flip(x, "row", size, bit))
        bit *= 2
    return x


def is_end(row):
    return (row == 0) | (row == 3)


def slots(owner_ref, panels):
    owners = [owner_ref[p] for p in range(panels)]
    out = []
    for p in range(panels):
        place = jnp.int32(0)
        for before in range(p):
            place = place + (owners[before] == owners[p]).astype(jnp.int32)
        out.append((owners[p], place))
    return out


def pack_kernel(ends, middles, owner_ref, coef_ref, basis_ref, mid_ref, low_ref, high_ref, sem):
    panels, rmax, width = coef_ref.shape
    half = rmax // 2
    full = width + basis_ref.shape[2]
    me = lax.axis_index("row")
    end = is_end(me)
    jobs = []
    for p, (owner, place) in enumerate(slots(owner_ref, panels)):
        mine = owner == me
        at_end = mine & end & (place < ends)
        at_mid = mine & jnp.logical_not(end) & (place < middles)
        for n, (src, lanes) in enumerate(((coef_ref, pl.ds(0, width)), (basis_ref, pl.ds(width, full - width)))):
            jobs.append((at_mid, pltpu.make_async_copy(src.at[p], mid_ref.at[place, :, lanes], sem.at[p, n])))
            for m, dst in enumerate((low_ref, high_ref)):
                rows = pl.ds(m * half, half)
                jobs.append((at_end, pltpu.make_async_copy(src.at[p, rows], dst.at[place, :, lanes], sem.at[p, 2 * m + n])))
    for when, copy in jobs:
        pl.when(when)(copy.start)
    for when, copy in jobs:
        pl.when(when)(copy.wait)


def pack(plan, owner, coef, basis):
    ends, middles = plan
    panels, rmax, width = coef.shape
    full = width + basis.shape[2]
    return pl.pallas_call(
        functools.partial(pack_kernel, ends, middles),
        out_shape=(
            jax.ShapeDtypeStruct((middles, rmax, full), coef.dtype),
            jax.ShapeDtypeStruct((ends, rmax // 2, full), coef.dtype),
            jax.ShapeDtypeStruct((ends, rmax // 2, full), coef.dtype),
        ),
        in_specs=[
            pl.BlockSpec(memory_space=pltpu.SMEM),
            pl.BlockSpec(memory_space=pl.ANY),
            pl.BlockSpec(memory_space=pl.ANY),
        ],
        out_specs=[pl.BlockSpec(memory_space=pl.ANY)] * 3,
        scratch_shapes=[pltpu.SemaphoreType.DMA((panels, 4))],
        cost_estimate=pl.CostEstimate(flops=0, bytes_accessed=1 << 20, transcendentals=0),
        name="pack_own_panels",
    )(owner, coef, basis)


def finish_kernel(gathered, owner_ref, lrank, lscale, rrank, rscale, *refs):
    came = refs[:gathered]
    coef_ref, basis_ref, held_ref, other_ref, block_ref, out_ref, right, high, low, sem = refs[gathered:]
    panels, rmax, width = coef_ref.shape
    wide = basis_ref.shape[2]
    half = rmax // 2
    cols = block_ref.shape[0]
    me = lax.axis_index("row")
    jobs = []

    def own(p):
        return [
            pltpu.make_async_copy(coef_ref.at[p], right.at[p, :, pl.ds(0, width)], sem.at[p, 0]),
            pltpu.make_async_copy(basis_ref.at[p], right.at[p, :, pl.ds(width, wide)], sem.at[p, 1]),
        ]

    if gathered:
        end = is_end(me)
        mid = jnp.logical_not(end)
        out1, in_low, in_high, across, far_low, far_high, out2, out_low, out_high = came
        for p, (owner, place) in enumerate(slots(owner_ref, panels)):
            apart = owner ^ me

            def whole(src):
                return [pltpu.make_async_copy(src.at[place], right.at[p], sem.at[p, 0])]

            def halves(one, two):
                return [
                    pltpu.make_async_copy(one.at[place], right.at[p, pl.ds(0, half)], sem.at[p, 0]),
                    pltpu.make_async_copy(two.at[place], right.at[p, pl.ds(half, half)], sem.at[p, 1]),
                ]

            for when, copies in (
                (apart == 0, own(p)),
                (end & (apart == 1), whole(out1)),
                (end & (apart == 2), whole(out2)),
                (end & (apart == 3), halves(out_low, out_high)),
                (mid & (apart == 1), halves(in_low, in_high)),
                (mid & (apart == 3), whole(across)),
                (mid & (apart == 2), halves(far_low, far_high)),
            ):
                jobs += [(when, copy) for copy in copies]
    else:
        for p in range(panels):
            jobs += [(jnp.bool_(True), copy) for copy in own(p)]
    for when, copy in jobs:
        pl.when(when)(copy.start)
    for when, copy in jobs:
        pl.when(when)(copy.wait)

    core_id = lax.axis_index("col") & 1
    row_at = lax.broadcasted_iota(jnp.int32, (rmax, rmax), 0)
    col_at = lax.broadcasted_iota(jnp.int32, (rmax, rmax), 1)
    per = held_ref.shape[0]
    for p in range(panels):
        mine = core_id == p // per
        left = jnp.where(mine, held_ref[p % per], other_ref[p % per])
        core = lax.dot_general(
            left[:, cols:], right[p, :, :width], (((1,), (1,)), ((), ())), preferred_element_type=jnp.float32
        )
        keep = (row_at < lrank[p, 0]) & (col_at < rrank[p, 0])
        core = jnp.where(keep, core * (lscale[p, 0] * rscale[p, 0]), 0.0)
        top = core.astype(jnp.bfloat16)
        rest = (core - top.astype(jnp.float32)).astype(jnp.bfloat16)
        basis = left[:, :cols]
        tall = lax.dot_general(
            jnp.concatenate([basis, basis], axis=0),
            jnp.concatenate([top, rest], axis=0),
            (((0,), (0,)), ((), ())),
            preferred_element_type=jnp.float32,
        )
        top = tall.astype(jnp.bfloat16)
        high[:, pl.ds(p * rmax, rmax)] = top
        low[:, pl.ds(p * rmax, rmax)] = (tall - top.astype(jnp.float32)).astype(jnp.bfloat16)
    flat = right[:, :, width:].reshape(panels * rmax, wide)
    update = jnp.dot(high[...], flat, preferred_element_type=jnp.float32)
    update = update + jnp.dot(low[...], flat, preferred_element_type=jnp.float32)
    out_ref[...] = block_ref[...] - update


def finish(came, owner, ranks, coef, basis, held, other, block):
    panels, rmax, width = coef.shape
    rows, wide = block.shape
    smem = pl.BlockSpec(memory_space=pltpu.SMEM)
    vmem = pl.BlockSpec(memory_space=pltpu.VMEM)
    anywhere = pl.BlockSpec(memory_space=pl.ANY)
    return pl.pallas_call(
        functools.partial(finish_kernel, len(came)),
        out_shape=jax.ShapeDtypeStruct(block.shape, block.dtype),
        in_specs=[smem] * 5 + [anywhere] * (len(came) + 2) + [vmem] * 3,
        out_specs=vmem,
        scratch_shapes=[
            pltpu.VMEM((panels, rmax, width + wide), coef.dtype),
            pltpu.VMEM((rows, panels * rmax), coef.dtype),
            pltpu.VMEM((rows, panels * rmax), coef.dtype),
            pltpu.SemaphoreType.DMA((panels, 2)),
        ],
        compiler_params=pltpu.CompilerParams(vmem_limit_bytes=24 << 20),
        cost_estimate=pl.CostEstimate(flops=1 << 29, bytes_accessed=4 << 20, transcendentals=0),
        name="apply_update",
    )(owner, *ranks, *came, coef, basis, held, other, block)


def planned(plan, size, block, lbasis, lcoef, rcoef, rbasis, ranks, lowner, rowner):
    mid, low, high = pack(plan, rowner, rcoef, rbasis)
    out1 = lax.ppermute(mid, "row", OUTWARD)
    across = lax.ppermute(mid, "row", MIDDLE)
    in_low = lax.ppermute(low, "row", INWARD)
    in_high = lax.ppermute(high, "row", INWARD)
    far_low = lax.ppermute(in_low, "row", MIDDLE)
    far_high = lax.ppermute(in_high, "row", MIDDLE)
    out2 = lax.ppermute(across, "row", OUTWARD)
    out_low = lax.ppermute(far_low, "row", OUTWARD)
    out_high = lax.ppermute(far_high, "row", OUTWARD)
    held, other = spread_left(lbasis, lcoef, lowner, size[1])
    came = (out1, in_low, in_high, across, far_low, far_high, out2, out_low, out_high)
    return finish(came, rowner, ranks, rcoef, rbasis, held, other, block)


def unplanned(size, block, lbasis, lcoef, rcoef, rbasis, ranks, lowner, rowner):
    rcoef = spread_right(rcoef, rowner, size[0])
    rbasis = spread_right(rbasis, rowner, size[0])
    held, other = spread_left(lbasis, lcoef, lowner, size[1])
    return finish((), rowner, ranks, rcoef, rbasis, held, other, block)


def shards(size, block, lbasis, lcoef, rcoef, rbasis, lrank, lscale, rrank, rscale, lowner, rowner):
    lbasis, lcoef, rcoef, rbasis = (x[:, 0] for x in (lbasis, lcoef, rcoef, rbasis))
    args = (block, lbasis, lcoef, rcoef, rbasis, (lrank, lscale, rrank, rscale), lowner, rowner)
    general = functools.partial(unplanned, size)
    if size[0] != 4:
        return general(*args)
    held = [jnp.sum((rowner == row).astype(jnp.int32)) for row in range(4)]
    ends, middles = jnp.maximum(held[0], held[3]), jnp.maximum(held[1], held[2])
    choice = jnp.int32(len(PLANS))
    for n, plan in reversed(list(enumerate(PLANS))):
        choice = jnp.where((ends <= plan[0]) & (middles <= plan[1]), n, choice)
    branches = [functools.partial(planned, plan, size) for plan in PLANS] + [general]
    return lax.switch(choice, branches, *args)


def solution(mesh):
    size = (mesh.shape["row"], mesh.shape["col"])
    return jax.shard_map(
        functools.partial(shards, size),
        mesh=mesh,
        in_specs=(
            P("row", "col"),
            P(None, "col", None, "row"),
            P(None, "col", None, "row"),
            P(None, "row", None, "col"),
            P(None, "row", None, "col"),
            P(None, "row"),
            P(None, "row"),
            P(None, "col"),
            P(None, "col"),
            P(),
            P(),
        ),
        out_specs=P("row", "col"),
        check_vma=False,
    )
```

```python
import functools

import jax
import jax.numpy as jnp
from jax import lax
from jax.experimental import pallas as pl
from jax.experimental.pallas import tpu as pltpu
from jax.sharding import PartitionSpec as P

ROOMS = (2, 3, 4, 5)
RING = ((0, 2), (2, 3), (3, 1), (1, 0))
BACK = tuple((to, start) for start, to in RING)


def flip(x, axis, size, bit):
    return lax.ppermute(x, axis, [(i, i ^ bit) for i in range(size)])


def same_bit(owner, me, bit):
    return ((owner & bit) == (me & bit))[:, None, None]


def carry_out(jobs):
    for when, copy in jobs:
        pl.when(when)(copy.start)
    for when, copy in jobs:
        pl.when(when)(copy.wait)


def halve_kernel(owner_ref, *refs):
    mine, came, (out, sem) = refs[:2], refs[2:4], refs[4:]
    me = lax.axis_index("col")
    count = out.shape[0]
    first = (me & 1) * count
    jobs = []
    for p in range(count):
        keep = (owner_ref[first + p] & 1) == (me & 1)
        lane = 0
        for n in range(2):
            width = mine[n].shape[2]
            for when, src in ((keep, mine[n]), (jnp.logical_not(keep), came[n])):
                jobs.append((when, pltpu.make_async_copy(src.at[first + p], out.at[p, :, pl.ds(lane, width)], sem.at[p, n])))
            lane += width
    carry_out(jobs)


def chip_kernel(owner_ref, *refs):
    came, (out, sem) = refs[:-2], refs[-2:]
    me = lax.axis_index("col")
    count = out.shape[0]
    jobs = []
    for p in range(count):
        apart = (owner_ref[(me & 1) * count + p] ^ me) >> 1
        for n, src in enumerate(came):
            jobs.append((apart == n, pltpu.make_async_copy(src.at[p], out.at[p], sem.at[p])))
    carry_out(jobs)


def choose(kernel, owner, came, shape, sems, name):
    return pl.pallas_call(
        kernel,
        out_shape=jax.ShapeDtypeStruct(shape, came[0].dtype),
        in_specs=[pl.BlockSpec(memory_space=pltpu.SMEM)] + [pl.BlockSpec(memory_space=pl.ANY)] * len(came),
        out_specs=pl.BlockSpec(memory_space=pltpu.VMEM),
        scratch_shapes=[pltpu.SemaphoreType.DMA(sems)],
        cost_estimate=pl.CostEstimate(flops=0, bytes_accessed=1 << 20, transcendentals=0),
        name=name,
    )(owner, *came)


def merge_cores(basis, coef, came, owner):
    panels, rmax, rows = basis.shape
    count = panels // 2
    shape = (count, rmax, rows + coef.shape[2])
    return choose(halve_kernel, owner, (basis, coef, *came), shape, (count, 2), "merge_cores")


def collect_left(held, owner, size):
    came = [flip(held, "col", size, bit) for bit in range(2, size, 2)]
    return choose(chip_kernel, owner, (held, *came), held.shape, held.shape[:1], "choose_chip")


def spread_right(x, owner, size):
    me = lax.axis_index("row")
    bit = 1
    while bit < size:
        x = jnp.where(same_bit(owner, me, bit), x, flip(x, "row", size, bit))
        bit *= 2
    return x


def slots(owner_ref, panels):
    owners = [owner_ref[p] for p in range(panels)]
    out = []
    for p in range(panels):
        place = jnp.int32(0)
        for before in range(p):
            place = place + (owners[before] == owners[p]).astype(jnp.int32)
        out.append((owners[p], place))
    return out


def pack_kernel(owner_ref, coef_ref, basis_ref, out_ref, sem):
    panels, rmax, width = coef_ref.shape
    room, _, full = out_ref.shape
    me = lax.axis_index("row")
    jobs = []
    for p, (owner, place) in enumerate(slots(owner_ref, panels)):
        mine = (owner == me) & (place < room)
        for n, (src, lanes) in enumerate(((coef_ref, pl.ds(0, width)), (basis_ref, pl.ds(width, full - width)))):
            jobs.append((mine, pltpu.make_async_copy(src.at[p], out_ref.at[place, :, lanes], sem.at[p, n])))
    carry_out(jobs)


def pack(room, owner, coef, basis):
    panels, rmax, width = coef.shape
    return pl.pallas_call(
        pack_kernel,
        out_shape=jax.ShapeDtypeStruct((room, rmax, width + basis.shape[2]), coef.dtype),
        in_specs=[
            pl.BlockSpec(memory_space=pltpu.SMEM),
            pl.BlockSpec(memory_space=pl.ANY),
            pl.BlockSpec(memory_space=pl.ANY),
        ],
        out_specs=pl.BlockSpec(memory_space=pltpu.VMEM),
        scratch_shapes=[pltpu.SemaphoreType.DMA((panels, 2))],
        cost_estimate=pl.CostEstimate(flops=0, bytes_accessed=1 << 20, transcendentals=0),
        name="pack_own_panels",
    )(owner, coef, basis)


def finish_kernel(gathered, owner_ref, lrank, lscale, rrank, rscale, *refs):
    came = refs[:gathered]
    coef_ref, basis_ref, held_ref, other_ref, block_ref, out_ref, right, left, block, high, low, sem, side_sem = refs[gathered:]
    panels, rmax, width = coef_ref.shape
    wide = basis_ref.shape[2]
    cols = block_ref.shape[0]
    me = lax.axis_index("row")
    core_id = lax.axis_index("col") & 1
    per = held_ref.shape[0]
    sides = [
        pltpu.make_async_copy(held_ref, left.at[pl.ds(core_id * per, per)], side_sem.at[0]),
        pltpu.make_async_copy(other_ref, left.at[pl.ds((1 - core_id) * per, per)], side_sem.at[1]),
        pltpu.make_async_copy(block_ref, block, side_sem.at[2]),
    ]
    jobs = []

    def own(p):
        return [
            pltpu.make_async_copy(coef_ref.at[p], right.at[p, :, pl.ds(0, width)], sem.at[p, 0]),
            pltpu.make_async_copy(basis_ref.at[p], right.at[p, :, pl.ds(width, wide)], sem.at[p, 1]),
        ]

    if gathered:
        ring, back, far = came
        near = jnp.where((me == 0) | (me == 3), 1, 2)
        for p, (owner, place) in enumerate(slots(owner_ref, panels)):
            apart = owner ^ me
            jobs += [(apart == 0, copy) for copy in own(p)]
            for when, src in ((apart == near, ring), (apart == 3 - near, back), (apart == 3, far)):
                jobs.append((when, pltpu.make_async_copy(src.at[place], right.at[p], sem.at[p, 0])))
    else:
        for p in range(panels):
            jobs += [(jnp.bool_(True), copy) for copy in own(p)]
    for copy in sides[:2]:
        copy.start()
    for when, copy in jobs:
        pl.when(when)(copy.start)
    sides[2].start()
    for copy in sides[:2]:
        copy.wait()
    for when, copy in jobs:
        pl.when(when)(copy.wait)

    row_at = lax.broadcasted_iota(jnp.int32, (rmax, rmax), 0)
    col_at = lax.broadcasted_iota(jnp.int32, (rmax, rmax), 1)
    for p in range(panels):
        core = lax.dot_general(
            left[p, :, cols:], right[p, :, :width], (((1,), (1,)), ((), ())), preferred_element_type=jnp.float32
        )
        keep = (row_at < lrank[p, 0]) & (col_at < rrank[p, 0])
        core = jnp.where(keep, core * (lscale[p, 0] * rscale[p, 0]), 0.0)
        top = core.astype(jnp.bfloat16)
        rest = (core - top.astype(jnp.float32)).astype(jnp.bfloat16)
        basis = left[p, :, :cols]
        tall = lax.dot_general(
            jnp.concatenate([basis, basis], axis=0),
            jnp.concatenate([top, rest], axis=0),
            (((0,), (0,)), ((), ())),
            preferred_element_type=jnp.float32,
        )
        top = tall.astype(jnp.bfloat16)
        high[:, pl.ds(p * rmax, rmax)] = top
        low[:, pl.ds(p * rmax, rmax)] = (tall - top.astype(jnp.float32)).astype(jnp.bfloat16)
    flat = right[:, :, width:].reshape(panels * rmax, wide)
    update = jnp.dot(high[...], flat, preferred_element_type=jnp.float32)
    update = update + jnp.dot(low[...], flat, preferred_element_type=jnp.float32)
    sides[2].wait()
    out_ref[...] = block[...] - update


def finish(came, owner, ranks, coef, basis, held, other, block):
    panels, rmax, width = coef.shape
    rows, wide = block.shape
    smem = pl.BlockSpec(memory_space=pltpu.SMEM)
    anywhere = pl.BlockSpec(memory_space=pl.ANY)
    return pl.pallas_call(
        functools.partial(finish_kernel, len(came)),
        out_shape=jax.ShapeDtypeStruct(block.shape, block.dtype),
        in_specs=[smem] * 5 + [anywhere] * (len(came) + 5),
        out_specs=pl.BlockSpec(memory_space=pltpu.VMEM),
        scratch_shapes=[
            pltpu.VMEM((panels, rmax, width + wide), coef.dtype),
            pltpu.VMEM((panels, rmax, held.shape[2]), coef.dtype),
            pltpu.VMEM(block.shape, block.dtype),
            pltpu.VMEM((rows, panels * rmax), coef.dtype),
            pltpu.VMEM((rows, panels * rmax), coef.dtype),
            pltpu.SemaphoreType.DMA((panels, 2)),
            pltpu.SemaphoreType.DMA((3,)),
        ],
        compiler_params=pltpu.CompilerParams(vmem_limit_bytes=56 << 20),
        cost_estimate=pl.CostEstimate(flops=1 << 29, bytes_accessed=4 << 20, transcendentals=0),
        name="apply_update",
    )(owner, *ranks, *came, coef, basis, held, other, block)


def planned(room, size, block, lbasis, lcoef, lcame, lowner, rcoef, rbasis, ranks, rowner):
    own = pack(room, rowner, rcoef, rbasis)
    lcame, own = lax.optimization_barrier((lcame, own))
    ring = lax.ppermute(own, "row", RING)
    back = lax.ppermute(own, "row", BACK)
    far = lax.ppermute(ring, "row", RING)
    held = collect_left(merge_cores(lbasis, lcoef, lcame, lowner), lowner, size[1])
    held, back = lax.optimization_barrier((held, back))
    other = flip(held, "col", size[1], 1)
    return finish((ring, back, far), rowner, ranks, rcoef, rbasis, held, other, block)


def unplanned(size, block, lbasis, lcoef, lcame, lowner, rcoef, rbasis, ranks, rowner):
    rcoef = spread_right(rcoef, rowner, size[0])
    rbasis = spread_right(rbasis, rowner, size[0])
    held = collect_left(merge_cores(lbasis, lcoef, lcame, lowner), lowner, size[1])
    other = flip(held, "col", size[1], 1)
    return finish((), rowner, ranks, rcoef, rbasis, held, other, block)


def plan_of(owner):
    held = jnp.sum((owner[None, :] == lax.broadcasted_iota(jnp.int32, (4, owner.shape[0]), 0)).astype(jnp.int32), axis=1)
    full = jnp.zeros(held.shape, jnp.int32)
    for n, room in enumerate(ROOMS):
        full = jnp.where(held > room, n + 1, full)
    return jnp.max(full)


def shards(size, block, lbasis, lcoef, rcoef, rbasis, lrank, lscale, rrank, rscale, lowner, rowner):
    lbasis, lcoef, rcoef, rbasis = (x[:, 0] for x in (lbasis, lcoef, rcoef, rbasis))
    lcame = tuple(flip(x, "col", size[1], 1) for x in (lbasis, lcoef))
    args = (block, lbasis, lcoef, lcame, lowner, rcoef, rbasis, (lrank, lscale, rrank, rscale), rowner)
    general = functools.partial(unplanned, size)
    if size[0] != 4:
        return general(*args)
    branches = [functools.partial(planned, room, size) for room in ROOMS] + [general]
    return lax.switch(plan_of(rowner), branches, *args)


def solution(mesh):
    size = (mesh.shape["row"], mesh.shape["col"])
    return jax.shard_map(
        functools.partial(shards, size),
        mesh=mesh,
        in_specs=(
            P("row", "col"),
            P(None, "col", None, "row"),
            P(None, "col", None, "row"),
            P(None, "row", None, "col"),
            P(None, "row", None, "col"),
            P(None, "row"),
            P(None, "row"),
            P(None, "col"),
            P(None, "col"),
            P(),
            P(),
        ),
        out_specs=P("row", "col"),
        check_vma=False,
    )
```

```python
import functools

import jax
import jax.numpy as jnp
from jax import lax
from jax.experimental import pallas as pl
from jax.experimental.pallas import tpu as pltpu
from jax.sharding import PartitionSpec as P

ROOM = 3
MORE = (1, 2, 5)
RING = ((0, 2), (2, 3), (3, 1), (1, 0))
BACK = tuple((to, start) for start, to in RING)

SMEM = pl.BlockSpec(memory_space=pltpu.SMEM)
VMEM = pl.BlockSpec(memory_space=pltpu.VMEM)
ANY = pl.BlockSpec(memory_space=pl.ANY)


def flip(x, axis, size, bit):
    return lax.ppermute(x, axis, [(i, i ^ bit) for i in range(size)])


def places(owners):
    out = []
    for p, owner in enumerate(owners):
        place = jnp.int32(0)
        for before in owners[:p]:
            place = place + (before == owner).astype(jnp.int32)
        out.append((owner, place))
    return out


def panels_of(owners, owner, first, room):
    panel_at = [jnp.int32(0)] * room
    count = jnp.int32(-first)
    for p, other in enumerate(owners):
        for n in range(room):
            panel_at[n] = jnp.where((other == owner) & (count == n), p, panel_at[n])
        count = count + (other == owner).astype(jnp.int32)
    return panel_at, count


def owners_of(owner_ref, shift=0):
    return [owner_ref[p] >> shift for p in range(owner_ref.shape[0])]


def table_of(rowner, lowner, lrank, lscale, rrank, rscale):
    return jnp.stack([rowner, lowner, rrank[:, 0], lrank[:, 0]]), lscale[:, 0] * rscale[:, 0]


def read_table(table_ref):
    return [[table_ref[n, p] for p in range(table_ref.shape[1])] for n in range(table_ref.shape[0])]


def call(kernel, name, out, specs, scratch, args, megabytes=1, flops=0):
    return pl.pallas_call(
        kernel,
        out_shape=out,
        in_specs=specs,
        out_specs=jax.tree.map(lambda _: VMEM, out),
        scratch_shapes=scratch,
        compiler_params=pltpu.CompilerParams(vmem_limit_bytes=24 << 20),
        cost_estimate=pl.CostEstimate(flops=flops, bytes_accessed=megabytes << 20, transcendentals=0),
        name=name,
    )(*args)


def left_kernel(owner_ref, basis_ref, coef_ref, basis_came, coef_came, out_ref, sem):
    me = lax.axis_index("col")
    room = out_ref.shape[0]
    rows = basis_ref.shape[2]
    lanes = pl.ds(0, rows), pl.ds(rows, out_ref.shape[2] - rows)
    owners = owners_of(owner_ref, 1)
    sources = (basis_ref, coef_ref), (basis_came, coef_came)
    panel_at, _ = panels_of(owners, me >> 1, 0, 2 * room)
    jobs = []
    for n in range(room):
        p = jnp.where((me & 1) == 0, panel_at[n], panel_at[n + room])
        mine = owner_ref[p] == me
        for when, pair in ((mine, sources[0]), (jnp.logical_not(mine), sources[1])):
            jobs.append((when, [pltpu.make_async_copy(pair[m].at[p], out_ref.at[n, :, lanes[m]], sem.at[n, m]) for m in range(2)]))
    for when, copies in jobs:
        pl.when(when)(lambda copies=copies: [copy.start() for copy in copies] and None)
    for _, copies in jobs[::2]:
        for copy in copies:
            copy.wait()


def spread_left(basis, coef, came, owner, size, after=None):
    panels, rmax, rows = basis.shape
    share = call(
        left_kernel,
        "share_left",
        jax.ShapeDtypeStruct((panels // 2, rmax, rows + coef.shape[2]), basis.dtype),
        [SMEM] + [ANY] * 4,
        [pltpu.SemaphoreType.DMA((panels // 2, 2))],
        (owner, basis, coef, *came),
    )
    mine = [share] + [flip(share, "col", size, bit) for bit in range(2, size, 2)]
    given = list(mine)
    if after is not None:
        given[1], after = lax.optimization_barrier((given[1], after))
    return [*mine, *(flip(x, "col", size, 1) for x in given)], after


def spread_right(x, owner, size):
    me = lax.axis_index("row")
    bit = 1
    while bit < size:
        keep = ((owner & bit) == (me & bit))[:, None, None]
        x = jnp.where(keep, x, flip(x, "row", size, bit))
        bit *= 2
    return x


def pack_kernel(first, owner_ref, coef_ref, basis_ref, out_ref, sem):
    width = coef_ref.shape[2]
    room, _, full = out_ref.shape
    lanes = pl.ds(0, width), pl.ds(width, full - width)
    panel_at, _ = panels_of(owners_of(owner_ref), lax.axis_index("row"), first, room)
    copies = []
    for n, p in enumerate(panel_at):
        for m, src in enumerate((coef_ref, basis_ref)):
            copies.append(pltpu.make_async_copy(src.at[p], out_ref.at[n, :, lanes[m]], sem.at[n, m]))
    for copy in copies:
        copy.start()
    for copy in copies:
        copy.wait()


def pack(first, room, owner, coef, basis):
    panels, rmax, width = coef.shape
    return call(
        functools.partial(pack_kernel, first),
        "pack_own_panels",
        jax.ShapeDtypeStruct((room, rmax, width + basis.shape[2]), coef.dtype),
        [SMEM, ANY, ANY],
        [pltpu.SemaphoreType.DMA((room, 2))],
        (owner, coef, basis),
    )


def split(x):
    high = x.astype(jnp.bfloat16)
    return high, (x - high.astype(jnp.float32)).astype(jnp.bfloat16)


def tall_tile(left, coef, lrank, rrank, scale):
    rmax = coef.shape[0]
    rows = left.shape[1] - coef.shape[1]
    core = lax.dot_general(left[:, rows:], coef, (((1,), (1,)), ((), ())), preferred_element_type=jnp.float32)
    at = [lax.broadcasted_iota(jnp.int32, (rmax, rmax), d) for d in range(2)]
    core = jnp.where((at[0] < lrank) & (at[1] < rrank), core * scale, 0.0)
    basis = left[:, :rows]
    tall = lax.dot_general(
        jnp.concatenate([basis, basis], axis=0),
        jnp.concatenate(split(core), axis=0),
        (((0,), (0,)), ((), ())),
        preferred_element_type=jnp.float32,
    )
    return split(tall)


def near_kernel(first, gathered, chips, table_ref, scale_ref, *refs):
    came, (coef_ref, basis_ref, block_ref), refs = refs[:gathered], refs[gathered : gathered + 3], refs[gathered + 3 :]
    sides, outs, (right, left, flat, high, low, sem) = refs[: 2 * chips], refs[2 * chips : -6], refs[-6:]
    out_ref = outs[0]
    panels, rmax, width = coef_ref.shape
    wide = basis_ref.shape[2]
    me, col = lax.axis_index("row"), lax.axis_index("col")
    per = sides[0].shape[0]
    room = came[0].shape[0] if gathered else 0
    pairs = [(src, left.at[n]) for n, src in enumerate(sides)]
    pairs += [(coef_ref, right.at[pl.ds(0, panels), :, pl.ds(0, width)]), (basis_ref, right.at[pl.ds(0, panels), :, pl.ds(width, wide)])]
    pairs += [(src, right.at[pl.ds(panels + n * room, room)]) for n, src in enumerate(came)]
    pairs += [(block_ref, out_ref)]
    copies = [pltpu.make_async_copy(src, dst, sem.at[n]) for n, (src, dst) in enumerate(pairs)]
    for copy in copies:
        copy.start()
    near = jnp.where((me == 0) | (me == 3), 1, 2)
    owners, lowners, rranks, lranks = read_table(table_ref)
    lefts = []
    for chip, place in places([owner >> 1 for owner in lowners]):
        core = (place // per != (col & 1)).astype(jnp.int32)
        lefts.append(((chip ^ (col >> 1)) + chips * core, lax.rem(place, per)))
    for copy in copies[:-1]:
        copy.wait()
    for p, (owner, place) in enumerate(places(owners)):
        if gathered:
            apart = owner ^ me
            source = jnp.where(apart == near, 0, jnp.where(apart == 3, 2, 1))
            here = (apart != 0) & (source < gathered) & (place >= first) & (place < first + room)
            at = jnp.where(here, panels + source * room + place - first, p)
            rrank_p = jnp.where(here | ((apart == 0) & (first == 0)), rranks[p], 0)
        else:
            at, rrank_p = p, rranks[p]
        tile = right[at]
        columns = pl.ds(p * rmax, rmax)
        high[:, columns], low[:, columns] = tall_tile(left[lefts[p]], tile[:, :width], lranks[p], rrank_p, scale_ref[p])
        flat[columns] = tile[:, width:]
    update = jnp.dot(high[...], flat[...], preferred_element_type=jnp.float32)
    update = update + jnp.dot(low[...], flat[...], preferred_element_type=jnp.float32)
    copies[-1].wait()
    out_ref[...] = out_ref[...] - update
    if len(outs) > 1:
        for n, p in enumerate(panels_of(owners, 3 - me, 0, room)[0]):
            buffer, at = jnp.int32(0), jnp.int32(0)
            for q in range(panels):
                buffer = jnp.where(p == q, lefts[q][0], buffer)
                at = jnp.where(p == q, lefts[q][1], at)
            outs[1][n] = left[buffer, at]


def far_kernel(table_ref, scale_ref, far_ref, left_ref, block_ref, out_ref, right, left, high, low, sem):
    room, rmax, full = far_ref.shape
    width = full - block_ref.shape[1]
    pairs = (far_ref, right), (left_ref, left), (block_ref, out_ref)
    copies = [pltpu.make_async_copy(src, dst, sem.at[n]) for n, (src, dst) in enumerate(pairs)]
    for copy in copies:
        copy.start()
    owners = read_table(table_ref)[0]
    panel_at, count = panels_of(owners, 3 - lax.axis_index("row"), 0, room)
    for copy in copies[:2]:
        copy.wait()
    bases = []
    for n, p in enumerate(panel_at):
        rrank = jnp.where(n < count, table_ref[2, p], 0)
        columns = pl.ds(n * rmax, rmax)
        high[:, columns], low[:, columns] = tall_tile(left[n], right[n, :, :width], table_ref[3, p], rrank, scale_ref[p])
        bases.append(jnp.where(n < count, right[n, :, width:], jnp.zeros((), right.dtype)))
    flat = jnp.concatenate(bases, axis=0)
    update = jnp.dot(high[...], flat, preferred_element_type=jnp.float32)
    update = update + jnp.dot(low[...], flat, preferred_element_type=jnp.float32)
    copies[2].wait()
    out_ref[...] = out_ref[...] - update


def apply_near(first, came, table, coef, basis, sides, block):
    panels, rmax, width = coef.shape
    rows, wide = block.shape
    kind = coef.dtype
    room = came[0].shape[0] if came else 0
    out = [jax.ShapeDtypeStruct(block.shape, block.dtype)]
    if len(came) == 2:
        out.append(jax.ShapeDtypeStruct((room, *sides[0].shape[1:]), kind))
    return call(
        functools.partial(near_kernel, first, len(came), len(sides) // 2),
        "apply_near",
        out,
        [SMEM] * 2 + [ANY] * (len(came) + 3 + len(sides)),
        [
            pltpu.VMEM((panels + room * len(came), rmax, width + wide), kind),
            pltpu.VMEM((len(sides), *sides[0].shape), kind),
            pltpu.VMEM((panels * rmax, wide), kind),
            pltpu.VMEM((rows, panels * rmax), kind),
            pltpu.VMEM((rows, panels * rmax), kind),
            pltpu.SemaphoreType.DMA((len(sides) + len(came) + 3,)),
        ],
        (*table, *came, coef, basis, block, *sides),
        megabytes=4,
        flops=1 << 29,
    )


def apply_far(far, table, left, block):
    room, rmax, _ = far.shape
    rows = block.shape[0]
    return call(
        far_kernel,
        "apply_far",
        jax.ShapeDtypeStruct(block.shape, block.dtype),
        [SMEM] * 2 + [ANY] * 3,
        [
            pltpu.VMEM(far.shape, far.dtype),
            pltpu.VMEM(left.shape, left.dtype),
            pltpu.VMEM((rows, room * rmax), far.dtype),
            pltpu.VMEM((rows, room * rmax), far.dtype),
            pltpu.SemaphoreType.DMA((3,)),
        ],
        (*table, far, left, block),
        megabytes=3,
        flops=1 << 28,
    )


def apply_more(room, block, rowner, table, rcoef, rbasis, sides):
    own = pack(ROOM, room, rowner, rcoef, rbasis)
    ring = lax.ppermute(own, "row", RING)
    more = ring, lax.ppermute(own, "row", BACK), lax.ppermute(ring, "row", RING)
    return apply_near(ROOM, more, table, rcoef, rbasis, sides, block)[0]


def apply_no_more(block, *_):
    return block


def plan_of(owner):
    row = lax.broadcasted_iota(jnp.int32, (4, owner.shape[0]), 0)
    held = jnp.sum((owner[None, :] == row).astype(jnp.int32), axis=1)
    plan = jnp.zeros(held.shape, jnp.int32)
    for n, room in enumerate((0, *MORE[:-1])):
        plan = jnp.where(held > ROOM + room, n + 1, plan)
    return jnp.max(plan)


def shards(size, block, lbasis, lcoef, rcoef, rbasis, lrank, lscale, rrank, rscale, lowner, rowner):
    lbasis, lcoef, rcoef, rbasis = (x[:, 0] for x in (lbasis, lcoef, rcoef, rbasis))
    table = table_of(rowner, lowner, lrank, lscale, rrank, rscale)
    if size[0] != 4:
        lcame = tuple(flip(x, "col", size[1], 1) for x in (lbasis, lcoef))
        rcoef, rbasis = (spread_right(x, rowner, size[0]) for x in (rcoef, rbasis))
        sides, _ = spread_left(lbasis, lcoef, lcame, lowner, size[1])
        return apply_near(0, (), table, rcoef, rbasis, sides, block)[0]
    own = pack(0, ROOM, rowner, rcoef, rbasis)
    lbasis, lcoef, own = lax.optimization_barrier((lbasis, lcoef, own))
    lcame = tuple(flip(x, "col", size[1], 1) for x in (lbasis, lcoef))
    ring = lax.ppermute(own, "row", RING)
    back = lax.ppermute(own, "row", BACK)
    ring, table, plan = lax.optimization_barrier((ring, table, plan_of(rowner)))
    far = lax.ppermute(ring, "row", RING)
    sides, ring = spread_left(lbasis, lcoef, lcame, lowner, size[1], ring)
    plans = [apply_no_more, *(functools.partial(apply_more, room) for room in MORE)]
    block, lefts = apply_near(0, (ring, back), table, rcoef, rbasis, sides, block)
    block = lax.switch(plan, plans, block, rowner, table, rcoef, rbasis, sides)
    return apply_far(far, table, lefts, block)


def solution(mesh):
    size = (mesh.shape["row"], mesh.shape["col"])
    return jax.shard_map(
        functools.partial(shards, size),
        mesh=mesh,
        in_specs=(
            P("row", "col"),
            P(None, "col", None, "row"),
            P(None, "col", None, "row"),
            P(None, "row", None, "col"),
            P(None, "row", None, "col"),
            P(None, "row"),
            P(None, "row"),
            P(None, "col"),
            P(None, "col"),
            P(),
            P(),
        ),
        out_specs=P("row", "col"),
        check_vma=False,
    )
```

```python
import functools

import jax
import jax.numpy as jnp
from jax import lax
from jax.experimental import pallas as pl
from jax.experimental.pallas import tpu as pltpu
from jax.sharding import PartitionSpec as P

ROOM = 3
MORE = (1, 2, 5)
RING = ((0, 2), (2, 3), (3, 1), (1, 0))
BACK = tuple((to, start) for start, to in RING)

SMEM = pl.BlockSpec(memory_space=pltpu.SMEM)
VMEM = pl.BlockSpec(memory_space=pltpu.VMEM)
ANY = pl.BlockSpec(memory_space=pl.ANY)


def flip(x, axis, size, bit):
    return lax.ppermute(x, axis, [(i, i ^ bit) for i in range(size)])


def places(owners):
    out = []
    for p, owner in enumerate(owners):
        place = jnp.int32(0)
        for before in owners[:p]:
            place = place + (before == owner).astype(jnp.int32)
        out.append((owner, place))
    return out


def panels_of(owners, owner, first, room):
    panel_at = [jnp.int32(0)] * room
    count = jnp.int32(-first)
    for p, other in enumerate(owners):
        for n in range(room):
            panel_at[n] = jnp.where((other == owner) & (count == n), p, panel_at[n])
        count = count + (other == owner).astype(jnp.int32)
    return panel_at, count


def owners_of(owner_ref, shift=0):
    return [owner_ref[p] >> shift for p in range(owner_ref.shape[0])]


def table_of(rowner, lowner, lrank, lscale, rrank, rscale, plan):
    plans = jnp.broadcast_to(plan, rowner.shape)
    return jnp.stack([rowner, lowner, rrank[:, 0], lrank[:, 0], plans]), lscale[:, 0] * rscale[:, 0]


def read_table(table_ref):
    return [[table_ref[n, p] for p in range(table_ref.shape[1])] for n in range(4)]


def call(kernel, name, out, specs, scratch, args, megabytes=1, flops=0, unused=()):
    return pl.pallas_call(
        kernel,
        out_shape=[*out, *unused],
        in_specs=specs,
        out_specs=[VMEM] * len(out) + [ANY] * len(unused),
        scratch_shapes=scratch,
        compiler_params=pltpu.CompilerParams(vmem_limit_bytes=24 << 20),
        cost_estimate=pl.CostEstimate(flops=flops, bytes_accessed=megabytes << 20, transcendentals=0),
        name=name,
    )(*args)


def left_kernel(owner_ref, basis_ref, coef_ref, basis_came, coef_came, out_ref, sem):
    me = lax.axis_index("col")
    room = out_ref.shape[0]
    rows = basis_ref.shape[2]
    lanes = pl.ds(0, rows), pl.ds(rows, out_ref.shape[2] - rows)
    owners = owners_of(owner_ref, 1)
    sources = (basis_ref, coef_ref), (basis_came, coef_came)
    panel_at, _ = panels_of(owners, me >> 1, 0, 2 * room)
    jobs = []
    for n in range(room):
        p = jnp.where((me & 1) == 0, panel_at[n], panel_at[n + room])
        mine = owner_ref[p] == me
        for when, pair in ((mine, sources[0]), (jnp.logical_not(mine), sources[1])):
            jobs.append((when, [pltpu.make_async_copy(pair[m].at[p], out_ref.at[n, :, lanes[m]], sem.at[n, m]) for m in range(2)]))
    for when, copies in jobs:
        pl.when(when)(lambda copies=copies: [copy.start() for copy in copies] and None)
    for _, copies in jobs[::2]:
        for copy in copies:
            copy.wait()


def share_left(basis, coef, came, owner):
    panels, rmax, rows = basis.shape
    return call(
        left_kernel,
        "share_left",
        [jax.ShapeDtypeStruct((panels // 2, rmax, rows + coef.shape[2]), basis.dtype)],
        [SMEM] + [ANY] * 4,
        [pltpu.SemaphoreType.DMA((panels // 2, 2))],
        (owner, basis, coef, *came),
    )[0]


def spread_left(share, size, after=None):
    mine = [share] + [flip(share, "col", size, bit) for bit in range(2, size, 2)]
    given = list(mine)
    if after is not None:
        given[0], after = lax.optimization_barrier((given[0], after))
    return [*mine, *(flip(x, "col", size, 1) for x in given)], after


def spread_right(x, owner, size):
    me = lax.axis_index("row")
    bit = 1
    while bit < size:
        keep = ((owner & bit) == (me & bit))[:, None, None]
        x = jnp.where(keep, x, flip(x, "row", size, bit))
        bit *= 2
    return x


def pack_kernel(first, owner_ref, coef_ref, basis_ref, out_ref, sem):
    width = coef_ref.shape[2]
    room, _, full = out_ref.shape
    lanes = pl.ds(0, width), pl.ds(width, full - width)
    panel_at, _ = panels_of(owners_of(owner_ref), lax.axis_index("row"), first, room)
    copies = []
    for n, p in enumerate(panel_at):
        for m, src in enumerate((coef_ref, basis_ref)):
            copies.append(pltpu.make_async_copy(src.at[p], out_ref.at[n, :, lanes[m]], sem.at[n, m]))
    for copy in copies:
        copy.start()
    for copy in copies:
        copy.wait()


def pack(first, room, owner, coef, basis):
    panels, rmax, width = coef.shape
    return call(
        functools.partial(pack_kernel, first),
        "pack_own_panels",
        [jax.ShapeDtypeStruct((room, rmax, width + basis.shape[2]), coef.dtype)],
        [SMEM, ANY, ANY],
        [pltpu.SemaphoreType.DMA((room, 2))],
        (owner, coef, basis),
    )[0]


def split(x):
    high = x.astype(jnp.bfloat16)
    return high, (x - high.astype(jnp.float32)).astype(jnp.bfloat16)


def tall_tile(left, coef, lrank, rrank, scale):
    rmax = coef.shape[0]
    rows = left.shape[1] - coef.shape[1]
    core = lax.dot_general(left[:, rows:], coef, (((1,), (1,)), ((), ())), preferred_element_type=jnp.float32)
    at = [lax.broadcasted_iota(jnp.int32, (rmax, rmax), d) for d in range(2)]
    core = jnp.where((at[0] < lrank) & (at[1] < rrank), core * scale, 0.0)
    basis = left[:, :rows]
    tall = lax.dot_general(
        jnp.concatenate([basis, basis], axis=0),
        jnp.concatenate(split(core), axis=0),
        (((0,), (0,)), ((), ())),
        preferred_element_type=jnp.float32,
    )
    return split(tall)


def near_kernel(first, gathered, chips, unused, table_ref, scale_ref, *refs):
    came, (coef_ref, basis_ref, block_ref), refs = refs[:gathered], refs[gathered : gathered + 3], refs[gathered + 3 :]
    sides, outs, (right, left, flat, high, low, sem) = refs[: 2 * chips], refs[2 * chips : -6], refs[-6:]
    outs = outs[: len(outs) - unused]
    out_ref = outs[0]
    panels, rmax, width = coef_ref.shape
    wide = basis_ref.shape[2]
    me, col = lax.axis_index("row"), lax.axis_index("col")
    per = sides[0].shape[0]
    room = came[0].shape[0] if gathered else 0
    pairs = [(src, left.at[n]) for n, src in enumerate(sides)]
    pairs += [(coef_ref, right.at[pl.ds(0, panels), :, pl.ds(0, width)]), (basis_ref, right.at[pl.ds(0, panels), :, pl.ds(width, wide)])]
    pairs += [(src, right.at[pl.ds(panels + n * room, room)]) for n, src in enumerate(came)]
    pairs += [(block_ref, out_ref)]
    copies = [pltpu.make_async_copy(src, dst, sem.at[n]) for n, (src, dst) in enumerate(pairs)]
    for copy in copies:
        copy.start()
    near = jnp.where((me == 0) | (me == 3), 1, 2)
    owners, lowners, rranks, lranks = read_table(table_ref)
    lefts = []
    for chip, place in places([owner >> 1 for owner in lowners]):
        core = (place // per != (col & 1)).astype(jnp.int32)
        lefts.append(((chip ^ (col >> 1)) + chips * core, lax.rem(place, per)))
    for copy in copies[:-1]:
        copy.wait()
    for p, (owner, place) in enumerate(places(owners)):
        if gathered:
            apart = owner ^ me
            source = jnp.where(apart == near, 0, jnp.where(apart == 3, 2, 1))
            here = (apart != 0) & (source < gathered) & (place >= first) & (place < first + room)
            at = jnp.where(here, panels + source * room + place - first, p)
            rrank_p = jnp.where(here | ((apart == 0) & (first == 0)), rranks[p], 0)
        else:
            at, rrank_p = p, rranks[p]
        tile = right[at]
        columns = pl.ds(p * rmax, rmax)
        high[:, columns], low[:, columns] = tall_tile(left[lefts[p]], tile[:, :width], lranks[p], rrank_p, scale_ref[p])
        flat[columns] = tile[:, width:]
    update = jnp.dot(high[...], flat[...], preferred_element_type=jnp.float32)
    update = update + jnp.dot(low[...], flat[...], preferred_element_type=jnp.float32)
    copies[-1].wait()
    out_ref[...] = out_ref[...] - update
    if len(outs) > 1:
        wanted = panels_of(owners, 3 - me, 0, room)[0]
        for apart in (near, 3 - near, 3):
            wanted += panels_of(owners, me ^ apart, room, 1)[0]
        for n, p in enumerate(wanted):
            buffer, at = jnp.int32(0), jnp.int32(0)
            for q in range(panels):
                buffer = jnp.where(p == q, lefts[q][0], buffer)
                at = jnp.where(p == q, lefts[q][1], at)
            outs[1][n] = left[buffer, at]


def far_kernel(table_ref, scale_ref, far_ref, left_ref, block_ref, *refs):
    *more, out_ref, right, high, low, sem = refs
    room, rmax, full = far_ref.shape
    width = full - block_ref.shape[1]
    me = lax.axis_index("row")
    near = jnp.where((me == 0) | (me == 3), 1, 2)
    owners = read_table(table_ref)[0]
    crowded = table_ref[4, 0] == 1
    extra = [pltpu.make_async_copy(src, right.at[pl.ds(n, 1)], sem.at[n]) for n, src in enumerate(more)]

    @pl.when(crowded)
    def _():
        for copy in extra:
            copy.start()

    def apply(first, panel_at, held, tiles):
        for n, p in enumerate(panel_at):
            rrank = jnp.where(held[n], table_ref[2, p], 0)
            columns = pl.ds((first + n) * rmax, rmax)
            high[:, columns], low[:, columns] = tall_tile(left_ref[first + n], tiles[n, :, :width], table_ref[3, p], rrank, scale_ref[p])
        columns = pl.ds(first * rmax, len(panel_at) * rmax)
        flat = tiles[:, :, width:].reshape(-1, full - width)
        update = jnp.dot(high[:, columns], flat, preferred_element_type=jnp.float32)
        return update + jnp.dot(low[:, columns], flat, preferred_element_type=jnp.float32)

    panel_at, count = panels_of(owners, 3 - me, 0, room)
    update = apply(0, panel_at, [n < count for n in range(room)], far_ref)
    out_ref[...] = block_ref[...] - update

    @pl.when(crowded)
    def _():
        for copy in extra:
            copy.wait()
        places_at = [panels_of(owners, me ^ apart, room, 1) for apart in (near, 3 - near, 3)]
        panel_at = [at[0] for at, _ in places_at]
        out_ref[...] = out_ref[...] - apply(room, panel_at, [count > 0 for _, count in places_at], right)


def apply_near(first, came, table, coef, basis, sides, block, unused=()):
    panels, rmax, width = coef.shape
    rows, wide = block.shape
    kind = coef.dtype
    room = came[0].shape[0] if came else 0
    out = [jax.ShapeDtypeStruct(block.shape, block.dtype)]
    if len(came) == 2:
        out.append(jax.ShapeDtypeStruct((room + 3, *sides[0].shape[1:]), kind))
    return call(
        functools.partial(near_kernel, first, len(came), len(sides) // 2, len(unused)),
        "apply_near",
        out,
        [SMEM] * 2 + [ANY] * (len(came) + 3 + len(sides)),
        [
            pltpu.VMEM((panels + room * len(came), rmax, width + wide), kind),
            pltpu.VMEM((len(sides), *sides[0].shape), kind),
            pltpu.VMEM((panels * rmax, wide), kind),
            pltpu.VMEM((rows, panels * rmax), kind),
            pltpu.VMEM((rows, panels * rmax), kind),
            pltpu.SemaphoreType.DMA((len(sides) + len(came) + 3,)),
        ],
        (*table, *came, coef, basis, block, *sides),
        megabytes=4,
        flops=1 << 29,
        unused=unused,
    )


def apply_far(far, table, left, block, more):
    room, rmax, full = far.shape
    rows = block.shape[0]
    slots = room + len(more)
    return call(
        far_kernel,
        "apply_far",
        [jax.ShapeDtypeStruct(block.shape, block.dtype)],
        [SMEM] * 2 + [VMEM] * 3 + [ANY] * len(more),
        [
            pltpu.VMEM((len(more), rmax, full), far.dtype),
            pltpu.VMEM((rows, slots * rmax), far.dtype),
            pltpu.VMEM((rows, slots * rmax), far.dtype),
            pltpu.SemaphoreType.DMA((len(more),)),
        ],
        (*table, far, left, block, *more),
        megabytes=3,
        flops=1 << 28,
    )[0]


def finish_near(room, block, ring, back, rowner, table, rcoef, rbasis, sides):
    one = jax.ShapeDtypeStruct((1, rcoef.shape[1], rcoef.shape[2] + rbasis.shape[2]), rcoef.dtype)
    if room:
        own = pack(ROOM, room, rowner, rcoef, rbasis)
        near = lax.ppermute(own, "row", RING), lax.ppermute(own, "row", BACK)
    block, lefts, *unused = apply_near(0, (ring, back), table, rcoef, rbasis, sides, block, () if room == 1 else (one,) * 3)
    if not room:
        return block, lefts, tuple(unused)
    ring, block = lax.optimization_barrier((near[0], block))
    more = *near, lax.ppermute(ring, "row", RING)
    if room == 1:
        return block, lefts, more
    return *apply_near(ROOM, more, table, rcoef, rbasis, sides, block), lefts, tuple(unused)


def plan_of(owner):
    row = lax.broadcasted_iota(jnp.int32, (4, owner.shape[0]), 0)
    held = jnp.sum((owner[None, :] == row).astype(jnp.int32), axis=1)
    plan = jnp.zeros(held.shape, jnp.int32)
    for n, room in enumerate((0, *MORE[:-1])):
        plan = jnp.where(held > ROOM + room, n + 1, plan)
    return jnp.max(plan)


def shards(size, block, lbasis, lcoef, rcoef, rbasis, lrank, lscale, rrank, rscale, lowner, rowner):
    lbasis, lcoef, rcoef, rbasis = (x[:, 0] for x in (lbasis, lcoef, rcoef, rbasis))
    plan = plan_of(rowner)
    table = table_of(rowner, lowner, lrank, lscale, rrank, rscale, plan)
    if size[0] != 4:
        lcame = tuple(flip(x, "col", size[1], 1) for x in (lbasis, lcoef))
        rcoef, rbasis = (spread_right(x, rowner, size[0]) for x in (rcoef, rbasis))
        sides, _ = spread_left(share_left(lbasis, lcoef, lcame, lowner), size[1])
        return apply_near(0, (), table, rcoef, rbasis, sides, block)[0]
    own = pack(0, ROOM, rowner, rcoef, rbasis)
    lbasis, lcoef, own = lax.optimization_barrier((lbasis, lcoef, own))
    lcame = tuple(flip(x, "col", size[1], 1) for x in (lbasis, lcoef))
    ring = lax.ppermute(own, "row", RING)
    share = share_left(lbasis, lcoef, lcame, lowner)
    share, own = lax.optimization_barrier((share, own))
    back = lax.ppermute(own, "row", BACK)
    ring, table, plan = lax.optimization_barrier((ring, table, plan))
    far = lax.ppermute(ring, "row", RING)
    sides, back = spread_left(share, size[1], back)
    plans = [functools.partial(finish_near, room) for room in (0, *MORE)]
    block, lefts, more = lax.switch(plan, plans, block, ring, back, rowner, table, rcoef, rbasis, sides)
    return apply_far(far, table, lefts, block, more)


def solution(mesh):
    size = (mesh.shape["row"], mesh.shape["col"])
    return jax.shard_map(
        functools.partial(shards, size),
        mesh=mesh,
        in_specs=(
            P("row", "col"),
            P(None, "col", None, "row"),
            P(None, "col", None, "row"),
            P(None, "row", None, "col"),
            P(None, "row", None, "col"),
            P(None, "row"),
            P(None, "row"),
            P(None, "col"),
            P(None, "col"),
            P(),
            P(),
        ),
        out_specs=P("row", "col"),
        check_vma=False,
    )
```

```python
import functools

import jax
import jax.numpy as jnp
from jax import lax
from jax.experimental import pallas as pl
from jax.experimental.pallas import tpu as pltpu
from jax.sharding import PartitionSpec as P

ROOM = 3
MORE = (1, 2, 5)
RING = ((0, 2), (2, 3), (3, 1), (1, 0))
BACK = tuple((to, start) for start, to in RING)

SMEM = pl.BlockSpec(memory_space=pltpu.SMEM)
VMEM = pl.BlockSpec(memory_space=pltpu.VMEM)
ANY = pl.BlockSpec(memory_space=pl.ANY)


def flip(x, axis, size, bit):
    return lax.ppermute(x, axis, [(i, i ^ bit) for i in range(size)])


def places(owners):
    out = []
    for p, owner in enumerate(owners):
        place = jnp.int32(0)
        for before in owners[:p]:
            place = place + (before == owner).astype(jnp.int32)
        out.append((owner, place))
    return out


def panels_of(owners, owner, first, room):
    panel_at = [jnp.int32(0)] * room
    count = jnp.int32(-first)
    for p, other in enumerate(owners):
        for n in range(room):
            panel_at[n] = jnp.where((other == owner) & (count == n), p, panel_at[n])
        count = count + (other == owner).astype(jnp.int32)
    return panel_at, count


def owners_of(owner_ref, shift=0):
    return [owner_ref[p] >> shift for p in range(owner_ref.shape[0])]


def table_of(rowner, lowner, lrank, lscale, rrank, rscale, plan):
    plans = jnp.broadcast_to(plan, rowner.shape)
    return jnp.stack([rowner, lowner, rrank[:, 0], lrank[:, 0], plans]), lscale[:, 0] * rscale[:, 0]


def read_table(table_ref):
    return [[table_ref[n, p] for p in range(table_ref.shape[1])] for n in range(4)]


def call(kernel, name, out, specs, scratch, args, megabytes=1, flops=0, unused=()):
    return pl.pallas_call(
        kernel,
        out_shape=[*out, *unused],
        in_specs=specs,
        out_specs=[VMEM] * len(out) + [ANY] * len(unused),
        scratch_shapes=scratch,
        compiler_params=pltpu.CompilerParams(vmem_limit_bytes=24 << 20),
        cost_estimate=pl.CostEstimate(flops=flops, bytes_accessed=megabytes << 20, transcendentals=0),
        name=name,
    )(*args)


def left_kernel(owner_ref, basis_ref, coef_ref, basis_came, coef_came, out_ref):
    me = lax.axis_index("col")
    room = out_ref.shape[0]
    rows = basis_ref.shape[2]
    panel_at, _ = panels_of(owners_of(owner_ref, 1), me >> 1, 0, 2 * room)
    for n in range(room):
        p = jnp.where((me & 1) == 0, panel_at[n], panel_at[n + room])
        mine = owner_ref[p] == me

        @pl.when(mine)
        def _():
            out_ref[n, :, :rows] = basis_ref[p]
            out_ref[n, :, rows:] = coef_ref[p]

        @pl.when(jnp.logical_not(mine))
        def _():
            out_ref[n, :, :rows] = basis_came[p]
            out_ref[n, :, rows:] = coef_came[p]


def share_left(basis, coef, came, owner):
    panels, rmax, rows = basis.shape
    return call(
        left_kernel,
        "share_left",
        [jax.ShapeDtypeStruct((panels // 2, rmax, rows + coef.shape[2]), basis.dtype)],
        [SMEM] + [VMEM] * 4,
        [],
        (owner, basis, coef, *came),
    )[0]


def spread_left(share, size, after=None):
    mine = [share] + [flip(share, "col", size, bit) for bit in range(2, size, 2)]
    given = list(mine)
    if after is not None:
        given[0], after = lax.optimization_barrier((given[0], after))
    return [*mine, *(flip(x, "col", size, 1) for x in given)], after


def spread_right(x, owner, size):
    me = lax.axis_index("row")
    bit = 1
    while bit < size:
        keep = ((owner & bit) == (me & bit))[:, None, None]
        x = jnp.where(keep, x, flip(x, "row", size, bit))
        bit *= 2
    return x


def pack_kernel(first, owner_ref, coef_ref, basis_ref, out_ref):
    width = coef_ref.shape[2]
    panel_at, _ = panels_of(owners_of(owner_ref), lax.axis_index("row"), first, out_ref.shape[0])
    for n, p in enumerate(panel_at):
        out_ref[n, :, :width] = coef_ref[p]
        out_ref[n, :, width:] = basis_ref[p]


def pack(first, room, owner, coef, basis):
    panels, rmax, width = coef.shape
    return call(
        functools.partial(pack_kernel, first),
        "pack_own_panels",
        [jax.ShapeDtypeStruct((room, rmax, width + basis.shape[2]), coef.dtype)],
        [SMEM, VMEM, VMEM],
        [],
        (owner, coef, basis),
    )[0]


def split(x):
    high = x.astype(jnp.bfloat16)
    return high, (x - high.astype(jnp.float32)).astype(jnp.bfloat16)


def tall_tile(left, coef, lrank, rrank, scale):
    rmax = coef.shape[0]
    rows = left.shape[1] - coef.shape[1]
    core = lax.dot_general(left[:, rows:], coef, (((1,), (1,)), ((), ())), preferred_element_type=jnp.float32)
    at = [lax.broadcasted_iota(jnp.int32, (rmax, rmax), d) for d in range(2)]
    core = jnp.where((at[0] < lrank) & (at[1] < rrank), core * scale, 0.0)
    basis = left[:, :rows]
    tall = lax.dot_general(
        jnp.concatenate([basis, basis], axis=0),
        jnp.concatenate(split(core), axis=0),
        (((0,), (0,)), ((), ())),
        preferred_element_type=jnp.float32,
    )
    return split(tall)


def near_kernel(first, gathered, chips, unused, table_ref, scale_ref, *refs):
    came, (coef_ref, basis_ref, block_ref), refs = refs[:gathered], refs[gathered : gathered + 3], refs[gathered + 3 :]
    sides, outs, (right, left, flat, high, low, sem) = refs[: 2 * chips], refs[2 * chips : -6], refs[-6:]
    outs = outs[: len(outs) - unused]
    out_ref = outs[0]
    panels, rmax, width = coef_ref.shape
    wide = basis_ref.shape[2]
    me, col = lax.axis_index("row"), lax.axis_index("col")
    per = sides[0].shape[0]
    room = came[0].shape[0] if gathered else 0
    pairs = [(src, left.at[n]) for n, src in enumerate(sides)]
    pairs += [(coef_ref, right.at[pl.ds(0, panels), :, pl.ds(0, width)]), (basis_ref, right.at[pl.ds(0, panels), :, pl.ds(width, wide)])]
    pairs += [(src, right.at[pl.ds(panels + n * room, room)]) for n, src in enumerate(came)]
    pairs += [(block_ref, out_ref)]
    copies = [pltpu.make_async_copy(src, dst, sem.at[n]) for n, (src, dst) in enumerate(pairs)]
    for copy in copies:
        copy.start()
    near = jnp.where((me == 0) | (me == 3), 1, 2)
    owners, lowners, rranks, lranks = read_table(table_ref)
    lefts = []
    for chip, place in places([owner >> 1 for owner in lowners]):
        core = (place // per != (col & 1)).astype(jnp.int32)
        lefts.append(((chip ^ (col >> 1)) + chips * core, lax.rem(place, per)))
    for copy in copies[:-1]:
        copy.wait()
    for p, (owner, place) in enumerate(places(owners)):
        if gathered:
            apart = owner ^ me
            source = jnp.where(apart == near, 0, jnp.where(apart == 3, 2, 1))
            here = (apart != 0) & (source < gathered) & (place >= first) & (place < first + room)
            at = jnp.where(here, panels + source * room + place - first, p)
            rrank_p = jnp.where(here | ((apart == 0) & (first == 0)), rranks[p], 0)
        else:
            at, rrank_p = p, rranks[p]
        tile = right[at]
        columns = pl.ds(p * rmax, rmax)
        high[:, columns], low[:, columns] = tall_tile(left[lefts[p]], tile[:, :width], lranks[p], rrank_p, scale_ref[p])
        flat[columns] = tile[:, width:]
    update = jnp.dot(high[...], flat[...], preferred_element_type=jnp.float32)
    update = update + jnp.dot(low[...], flat[...], preferred_element_type=jnp.float32)
    copies[-1].wait()
    out_ref[...] = out_ref[...] - update
    if len(outs) > 1:
        wanted = panels_of(owners, 3 - me, 0, room)[0]
        for apart in (near, 3 - near, 3):
            wanted += panels_of(owners, me ^ apart, room, 1)[0]
        for n, p in enumerate(wanted):
            buffer, at = jnp.int32(0), jnp.int32(0)
            for q in range(panels):
                buffer = jnp.where(p == q, lefts[q][0], buffer)
                at = jnp.where(p == q, lefts[q][1], at)
            outs[1][n] = left[buffer, at]


def far_kernel(table_ref, scale_ref, far_ref, left_ref, block_ref, *refs):
    *more, out_ref, right, high, low, sem = refs
    room, rmax, full = far_ref.shape
    width = full - block_ref.shape[1]
    me = lax.axis_index("row")
    near = jnp.where((me == 0) | (me == 3), 1, 2)
    owners = read_table(table_ref)[0]
    crowded = table_ref[4, 0] == 1
    extra = [pltpu.make_async_copy(src, right.at[pl.ds(n, 1)], sem.at[n]) for n, src in enumerate(more)]

    @pl.when(crowded)
    def _():
        for copy in extra:
            copy.start()

    def apply(first, panel_at, held, tiles):
        for n, p in enumerate(panel_at):
            rrank = jnp.where(held[n], table_ref[2, p], 0)
            columns = pl.ds((first + n) * rmax, rmax)
            high[:, columns], low[:, columns] = tall_tile(left_ref[first + n], tiles[n, :, :width], table_ref[3, p], rrank, scale_ref[p])
        columns = pl.ds(first * rmax, len(panel_at) * rmax)
        flat = tiles[:, :, width:].reshape(-1, full - width)
        update = jnp.dot(high[:, columns], flat, preferred_element_type=jnp.float32)
        return update + jnp.dot(low[:, columns], flat, preferred_element_type=jnp.float32)

    panel_at, count = panels_of(owners, 3 - me, 0, room)
    update = apply(0, panel_at, [n < count for n in range(room)], far_ref)
    out_ref[...] = block_ref[...] - update

    @pl.when(crowded)
    def _():
        for copy in extra:
            copy.wait()
        places_at = [panels_of(owners, me ^ apart, room, 1) for apart in (near, 3 - near, 3)]
        panel_at = [at[0] for at, _ in places_at]
        out_ref[...] = out_ref[...] - apply(room, panel_at, [count > 0 for _, count in places_at], right)


def apply_near(first, came, table, coef, basis, sides, block, unused=()):
    panels, rmax, width = coef.shape
    rows, wide = block.shape
    kind = coef.dtype
    room = came[0].shape[0] if came else 0
    out = [jax.ShapeDtypeStruct(block.shape, block.dtype)]
    if len(came) == 2:
        out.append(jax.ShapeDtypeStruct((room + 3, *sides[0].shape[1:]), kind))
    return call(
        functools.partial(near_kernel, first, len(came), len(sides) // 2, len(unused)),
        "apply_near",
        out,
        [SMEM] * 2 + [ANY] * (len(came) + 3 + len(sides)),
        [
            pltpu.VMEM((panels + room * len(came), rmax, width + wide), kind),
            pltpu.VMEM((len(sides), *sides[0].shape), kind),
            pltpu.VMEM((panels * rmax, wide), kind),
            pltpu.VMEM((rows, panels * rmax), kind),
            pltpu.VMEM((rows, panels * rmax), kind),
            pltpu.SemaphoreType.DMA((len(sides) + len(came) + 3,)),
        ],
        (*table, *came, coef, basis, block, *sides),
        megabytes=4,
        flops=1 << 29,
        unused=unused,
    )


def apply_far(far, table, left, block, more):
    room, rmax, full = far.shape
    rows = block.shape[0]
    slots = room + len(more)
    return call(
        far_kernel,
        "apply_far",
        [jax.ShapeDtypeStruct(block.shape, block.dtype)],
        [SMEM] * 2 + [VMEM] * 3 + [ANY] * len(more),
        [
            pltpu.VMEM((len(more), rmax, full), far.dtype),
            pltpu.VMEM((rows, slots * rmax), far.dtype),
            pltpu.VMEM((rows, slots * rmax), far.dtype),
            pltpu.SemaphoreType.DMA((len(more),)),
        ],
        (*table, far, left, block, *more),
        megabytes=3,
        flops=1 << 28,
    )[0]


def finish_near(room, block, ring, back, rowner, table, rcoef, rbasis, sides):
    one = jax.ShapeDtypeStruct((1, rcoef.shape[1], rcoef.shape[2] + rbasis.shape[2]), rcoef.dtype)
    if room:
        own = pack(ROOM, room, rowner, rcoef, rbasis)
        near = lax.ppermute(own, "row", RING), lax.ppermute(own, "row", BACK)
    block, lefts, *unused = apply_near(0, (ring, back), table, rcoef, rbasis, sides, block, () if room == 1 else (one,) * 3)
    if not room:
        return block, lefts, tuple(unused)
    ring, block = lax.optimization_barrier((near[0], block))
    more = *near, lax.ppermute(ring, "row", RING)
    if room == 1:
        return block, lefts, more
    return *apply_near(ROOM, more, table, rcoef, rbasis, sides, block), lefts, tuple(unused)


def plan_of(owner):
    row = lax.broadcasted_iota(jnp.int32, (4, owner.shape[0]), 0)
    held = jnp.sum((owner[None, :] == row).astype(jnp.int32), axis=1)
    plan = jnp.zeros(held.shape, jnp.int32)
    for n, room in enumerate((0, *MORE[:-1])):
        plan = jnp.where(held > ROOM + room, n + 1, plan)
    return jnp.max(plan)


def shards(size, block, lbasis, lcoef, rcoef, rbasis, lrank, lscale, rrank, rscale, lowner, rowner):
    lbasis, lcoef, rcoef, rbasis = (x[:, 0] for x in (lbasis, lcoef, rcoef, rbasis))
    plan = plan_of(rowner)
    table = table_of(rowner, lowner, lrank, lscale, rrank, rscale, plan)
    if size[0] != 4:
        lcame = tuple(flip(x, "col", size[1], 1) for x in (lbasis, lcoef))
        rcoef, rbasis = (spread_right(x, rowner, size[0]) for x in (rcoef, rbasis))
        sides, _ = spread_left(share_left(lbasis, lcoef, lcame, lowner), size[1])
        return apply_near(0, (), table, rcoef, rbasis, sides, block)[0]
    own = pack(0, ROOM, rowner, rcoef, rbasis)
    lbasis, lcoef, own = lax.optimization_barrier((lbasis, lcoef, own))
    lcame = tuple(flip(x, "col", size[1], 1) for x in (lbasis, lcoef))
    ring = lax.ppermute(own, "row", RING)
    share = share_left(lbasis, lcoef, lcame, lowner)
    share, own = lax.optimization_barrier((share, own))
    back = lax.ppermute(own, "row", BACK)
    ring, table, plan = lax.optimization_barrier((ring, table, plan))
    far = lax.ppermute(ring, "row", RING)
    sides, back = spread_left(share, size[1], back)
    plans = [functools.partial(finish_near, room) for room in (0, *MORE)]
    block, lefts, more = lax.switch(plan, plans, block, ring, back, rowner, table, rcoef, rbasis, sides)
    return apply_far(far, table, lefts, block, more)


def solution(mesh):
    size = (mesh.shape["row"], mesh.shape["col"])
    return jax.shard_map(
        functools.partial(shards, size),
        mesh=mesh,
        in_specs=(
            P("row", "col"),
            P(None, "col", None, "row"),
            P(None, "col", None, "row"),
            P(None, "row", None, "col"),
            P(None, "row", None, "col"),
            P(None, "row"),
            P(None, "row"),
            P(None, "col"),
            P(None, "col"),
            P(),
            P(),
        ),
        out_specs=P("row", "col"),
        check_vma=False,
    )
```

```python
import functools

import jax
import jax.numpy as jnp
from jax import lax
from jax.experimental import pallas as pl
from jax.experimental.pallas import tpu as pltpu
from jax.sharding import PartitionSpec as P

ROOM = 3
MORE = (1, 2, 5)
RING = ((0, 2), (2, 3), (3, 1), (1, 0))
BACK = tuple((to, start) for start, to in RING)

SMEM = pl.BlockSpec(memory_space=pltpu.SMEM)
VMEM = pl.BlockSpec(memory_space=pltpu.VMEM)
ANY = pl.BlockSpec(memory_space=pl.ANY)


def flip(x, axis, size, bit):
    return lax.ppermute(x, axis, [(i, i ^ bit) for i in range(size)])


def places(owners):
    out = []
    for p, owner in enumerate(owners):
        place = jnp.int32(0)
        for before in owners[:p]:
            place = place + (before == owner).astype(jnp.int32)
        out.append((owner, place))
    return out


def panels_of(owners, owner, first, room):
    panel_at = [jnp.int32(0)] * room
    count = jnp.int32(-first)
    for p, other in enumerate(owners):
        for n in range(room):
            panel_at[n] = jnp.where((other == owner) & (count == n), p, panel_at[n])
        count = count + (other == owner).astype(jnp.int32)
    return panel_at, count


def owners_of(owner_ref, shift=0):
    return [owner_ref[p] >> shift for p in range(owner_ref.shape[0])]


def table_of(rowner, lowner, lrank, lscale, rrank, rscale, plan):
    plans = jnp.broadcast_to(plan, rowner.shape)
    return jnp.stack([rowner, lowner, rrank[:, 0], lrank[:, 0], plans]), lscale[:, 0] * rscale[:, 0]


def read_table(table_ref):
    return [[table_ref[n, p] for p in range(table_ref.shape[1])] for n in range(4)]


def call(kernel, name, out, specs, scratch, args, megabytes=1, flops=0, unused=()):
    return pl.pallas_call(
        kernel,
        out_shape=[*out, *unused],
        in_specs=specs,
        out_specs=[VMEM] * len(out) + [ANY] * len(unused),
        scratch_shapes=scratch,
        compiler_params=pltpu.CompilerParams(vmem_limit_bytes=24 << 20),
        cost_estimate=pl.CostEstimate(flops=flops, bytes_accessed=megabytes << 20, transcendentals=0),
        name=name,
    )(*args)


def left_kernel(owner_ref, basis_ref, coef_ref, basis_came, coef_came, out_ref):
    me = lax.axis_index("col")
    room = out_ref.shape[0]
    rows = basis_ref.shape[2]
    panel_at, _ = panels_of(owners_of(owner_ref, 1), me >> 1, 0, 2 * room)
    for n in range(room):
        p = jnp.where((me & 1) == 0, panel_at[n], panel_at[n + room])
        mine = owner_ref[p] == me

        @pl.when(mine)
        def _():
            out_ref[n, :, :rows] = basis_ref[p]
            out_ref[n, :, rows:] = coef_ref[p]

        @pl.when(jnp.logical_not(mine))
        def _():
            out_ref[n, :, :rows] = basis_came[p]
            out_ref[n, :, rows:] = coef_came[p]


def share_left(basis, coef, came, owner):
    panels, rmax, rows = basis.shape
    return call(
        left_kernel,
        "share_left",
        [jax.ShapeDtypeStruct((panels // 2, rmax, rows + coef.shape[2]), basis.dtype)],
        [SMEM] + [VMEM] * 4,
        [],
        (owner, basis, coef, *came),
    )[0]


def spread_left(share, size, after=None):
    mine = [share] + [flip(share, "col", size, bit) for bit in range(2, size, 2)]
    given = list(mine)
    if after is not None:
        given[0], after = lax.optimization_barrier((given[0], after))
    return [*mine, *(flip(x, "col", size, 1) for x in given)], after


def spread_right(x, owner, size):
    me = lax.axis_index("row")
    bit = 1
    while bit < size:
        keep = ((owner & bit) == (me & bit))[:, None, None]
        x = jnp.where(keep, x, flip(x, "row", size, bit))
        bit *= 2
    return x


def pack_kernel(first, owner_ref, coef_ref, basis_ref, out_ref):
    width = coef_ref.shape[2]
    panel_at, _ = panels_of(owners_of(owner_ref), lax.axis_index("row"), first, out_ref.shape[0])
    for n, p in enumerate(panel_at):
        out_ref[n, :, :width] = coef_ref[p]
        out_ref[n, :, width:] = basis_ref[p]


def pack(first, room, owner, coef, basis):
    panels, rmax, width = coef.shape
    return call(
        functools.partial(pack_kernel, first),
        "pack_own_panels",
        [jax.ShapeDtypeStruct((room, rmax, width + basis.shape[2]), coef.dtype)],
        [SMEM, VMEM, VMEM],
        [],
        (owner, coef, basis),
    )[0]


def split(x):
    high = x.astype(jnp.bfloat16)
    return high, (x - high.astype(jnp.float32)).astype(jnp.bfloat16)


def wide_tile(left, coef, lrank, rrank, scale):
    rmax = coef.shape[0]
    rows = left.shape[1] - coef.shape[1]
    core = lax.dot_general(coef, left[:, rows:], (((1,), (1,)), ((), ())), preferred_element_type=jnp.float32)
    at = [lax.broadcasted_iota(jnp.int32, (rmax, rmax), d) for d in range(2)]
    core = jnp.where((at[1] < lrank) & (at[0] < rrank), core * scale, 0.0)
    basis = left[:, :rows]
    high, low = split(core)
    wide = jnp.dot(high, basis, preferred_element_type=jnp.float32)
    return split(wide + jnp.dot(low, basis, preferred_element_type=jnp.float32))


def turned_dot(x, y):
    return lax.dot_general(x, y, (((0,), (0,)), ((), ())), preferred_element_type=jnp.float32)


def near_kernel(first, gathered, chips, unused, table_ref, scale_ref, *refs):
    came, (coef_ref, basis_ref, block_ref), refs = refs[:gathered], refs[gathered : gathered + 3], refs[gathered + 3 :]
    sides, outs, (right, left, flat, high, low, sem) = refs[: 2 * chips], refs[2 * chips : -6], refs[-6:]
    outs = outs[: len(outs) - unused]
    out_ref = outs[0]
    panels, rmax, width = coef_ref.shape
    wide = basis_ref.shape[2]
    me, col = lax.axis_index("row"), lax.axis_index("col")
    per = sides[0].shape[0]
    room = came[0].shape[0] if gathered else 0
    pairs = [(src, left.at[n]) for n, src in enumerate(sides)]
    pairs += [(coef_ref, right.at[pl.ds(0, panels), :, pl.ds(0, width)]), (basis_ref, right.at[pl.ds(0, panels), :, pl.ds(width, wide)])]
    pairs += [(src, right.at[pl.ds(panels + n * room, room)]) for n, src in enumerate(came)]
    pairs += [(block_ref, out_ref)]
    copies = [pltpu.make_async_copy(src, dst, sem.at[n]) for n, (src, dst) in enumerate(pairs)]
    for copy in copies:
        copy.start()
    near = jnp.where((me == 0) | (me == 3), 1, 2)
    owners, lowners, rranks, lranks = read_table(table_ref)
    lefts = []
    for chip, place in places([owner >> 1 for owner in lowners]):
        core = (place // per != (col & 1)).astype(jnp.int32)
        lefts.append(((chip ^ (col >> 1)) + chips * core, lax.rem(place, per)))
    for copy in copies[:-1]:
        copy.wait()
    for p, (owner, place) in enumerate(places(owners)):
        if gathered:
            apart = owner ^ me
            source = jnp.where(apart == near, 0, jnp.where(apart == 3, 2, 1))
            here = (apart != 0) & (source < gathered) & (place >= first) & (place < first + room)
            at = jnp.where(here, panels + source * room + place - first, p)
            rrank_p = jnp.where(here | ((apart == 0) & (first == 0)), rranks[p], 0)
        else:
            at, rrank_p = p, rranks[p]
        tile = right[at]
        columns = pl.ds(p * rmax, rmax)
        high[columns], low[columns] = wide_tile(left[lefts[p]], tile[:, :width], lranks[p], rrank_p, scale_ref[p])
        flat[columns] = tile[:, width:]
    update = turned_dot(high[...], flat[...]) + turned_dot(low[...], flat[...])
    copies[-1].wait()
    out_ref[...] = out_ref[...] - update
    if len(outs) > 1:
        wanted = panels_of(owners, 3 - me, 0, room)[0]
        for apart in (near, 3 - near, 3):
            wanted += panels_of(owners, me ^ apart, room, 1)[0]
        for n, p in enumerate(wanted):
            buffer, at = jnp.int32(0), jnp.int32(0)
            for q in range(panels):
                buffer = jnp.where(p == q, lefts[q][0], buffer)
                at = jnp.where(p == q, lefts[q][1], at)
            outs[1][n] = left[buffer, at]


def far_kernel(table_ref, scale_ref, far_ref, left_ref, block_ref, *refs):
    *more, out_ref, right, high, low, sem = refs
    room, rmax, full = far_ref.shape
    width = full - block_ref.shape[1]
    me = lax.axis_index("row")
    near = jnp.where((me == 0) | (me == 3), 1, 2)
    owners = read_table(table_ref)[0]
    crowded = table_ref[4, 0] == 1
    extra = [pltpu.make_async_copy(src, right.at[pl.ds(n, 1)], sem.at[n]) for n, src in enumerate(more)]

    @pl.when(crowded)
    def _():
        for copy in extra:
            copy.start()

    def apply(first, panel_at, held, tiles):
        for n, p in enumerate(panel_at):
            rrank = jnp.where(held[n], table_ref[2, p], 0)
            columns = pl.ds((first + n) * rmax, rmax)
            high[columns], low[columns] = wide_tile(left_ref[first + n], tiles[n, :, :width], table_ref[3, p], rrank, scale_ref[p])
        columns = pl.ds(first * rmax, len(panel_at) * rmax)
        flat = tiles[:, :, width:].reshape(-1, full - width)
        return turned_dot(high[columns], flat) + turned_dot(low[columns], flat)

    def opposite():
        panel_at, count = panels_of(owners, 3 - me, 0, room)
        return apply(0, panel_at, [n < count for n in range(room)], far_ref)

    @pl.when(jnp.logical_not(crowded))
    def _():
        out_ref[...] = block_ref[...] - opposite()

    @pl.when(crowded)
    def _():
        update = opposite()
        places_at = [panels_of(owners, me ^ apart, room, 1) for apart in (near, 3 - near, 3)]
        panel_at = [at[0] for at, _ in places_at]
        for copy in extra:
            copy.wait()
        update = update + apply(room, panel_at, [count > 0 for _, count in places_at], right)
        out_ref[...] = block_ref[...] - update


def apply_near(first, came, table, coef, basis, sides, block, unused=()):
    panels, rmax, width = coef.shape
    rows, wide = block.shape
    kind = coef.dtype
    room = came[0].shape[0] if came else 0
    out = [jax.ShapeDtypeStruct(block.shape, block.dtype)]
    if len(came) == 2:
        out.append(jax.ShapeDtypeStruct((room + 3, *sides[0].shape[1:]), kind))
    return call(
        functools.partial(near_kernel, first, len(came), len(sides) // 2, len(unused)),
        "apply_near",
        out,
        [SMEM] * 2 + [ANY] * (len(came) + 3 + len(sides)),
        [
            pltpu.VMEM((panels + room * len(came), rmax, width + wide), kind),
            pltpu.VMEM((len(sides), *sides[0].shape), kind),
            pltpu.VMEM((panels * rmax, wide), kind),
            pltpu.VMEM((panels * rmax, rows), kind),
            pltpu.VMEM((panels * rmax, rows), kind),
            pltpu.SemaphoreType.DMA((len(sides) + len(came) + 3,)),
        ],
        (*table, *came, coef, basis, block, *sides),
        megabytes=4,
        flops=1 << 29,
        unused=unused,
    )


def apply_far(far, table, left, block, more):
    room, rmax, full = far.shape
    rows = block.shape[0]
    slots = room + len(more)
    return call(
        far_kernel,
        "apply_far",
        [jax.ShapeDtypeStruct(block.shape, block.dtype)],
        [SMEM] * 2 + [VMEM] * 3 + [ANY] * len(more),
        [
            pltpu.VMEM((len(more), rmax, full), far.dtype),
            pltpu.VMEM((slots * rmax, rows), far.dtype),
            pltpu.VMEM((slots * rmax, rows), far.dtype),
            pltpu.SemaphoreType.DMA((len(more),)),
        ],
        (*table, far, left, block, *more),
        megabytes=3,
        flops=1 << 28,
    )[0]


def finish_near(room, block, ring, back, rowner, table, rcoef, rbasis, sides):
    one = jax.ShapeDtypeStruct((1, rcoef.shape[1], rcoef.shape[2] + rbasis.shape[2]), rcoef.dtype)
    if room:
        own = pack(ROOM, room, rowner, rcoef, rbasis)
        near = lax.ppermute(own, "row", RING), lax.ppermute(own, "row", BACK)
    block, lefts, *unused = apply_near(0, (ring, back), table, rcoef, rbasis, sides, block, () if room == 1 else (one,) * 3)
    if not room:
        return block, lefts, tuple(unused)
    ring, block = lax.optimization_barrier((near[0], block))
    more = *near, lax.ppermute(ring, "row", RING)
    if room == 1:
        return block, lefts, more
    return *apply_near(ROOM, more, table, rcoef, rbasis, sides, block), lefts, tuple(unused)


def plan_of(owner):
    row = lax.broadcasted_iota(jnp.int32, (4, owner.shape[0]), 0)
    held = jnp.sum((owner[None, :] == row).astype(jnp.int32), axis=1)
    plan = jnp.zeros(held.shape, jnp.int32)
    for n, room in enumerate((0, *MORE[:-1])):
        plan = jnp.where(held > ROOM + room, n + 1, plan)
    return jnp.max(plan)


def shards(size, block, lbasis, lcoef, rcoef, rbasis, lrank, lscale, rrank, rscale, lowner, rowner):
    lbasis, lcoef, rcoef, rbasis = (x[:, 0] for x in (lbasis, lcoef, rcoef, rbasis))
    plan = plan_of(rowner)
    table = table_of(rowner, lowner, lrank, lscale, rrank, rscale, plan)
    if size[0] != 4:
        lcame = tuple(flip(x, "col", size[1], 1) for x in (lbasis, lcoef))
        rcoef, rbasis = (spread_right(x, rowner, size[0]) for x in (rcoef, rbasis))
        sides, _ = spread_left(share_left(lbasis, lcoef, lcame, lowner), size[1])
        return apply_near(0, (), table, rcoef, rbasis, sides, block)[0]
    own = pack(0, ROOM, rowner, rcoef, rbasis)
    lbasis, lcoef, own = lax.optimization_barrier((lbasis, lcoef, own))
    lcame = tuple(flip(x, "col", size[1], 1) for x in (lbasis, lcoef))
    ring = lax.ppermute(own, "row", RING)
    share = share_left(lbasis, lcoef, lcame, lowner)
    share, own = lax.optimization_barrier((share, own))
    back = lax.ppermute(own, "row", BACK)
    ring, table, plan = lax.optimization_barrier((ring, table, plan))
    far = lax.ppermute(ring, "row", RING)
    sides, back = spread_left(share, size[1], back)
    plans = [functools.partial(finish_near, room) for room in (0, *MORE)]
    block, lefts, more = lax.switch(plan, plans, block, ring, back, rowner, table, rcoef, rbasis, sides)
    return apply_far(far, table, lefts, block, more)


def solution(mesh):
    size = (mesh.shape["row"], mesh.shape["col"])
    return jax.shard_map(
        functools.partial(shards, size),
        mesh=mesh,
        in_specs=(
            P("row", "col"),
            P(None, "col", None, "row"),
            P(None, "col", None, "row"),
            P(None, "row", None, "col"),
            P(None, "row", None, "col"),
            P(None, "row"),
            P(None, "row"),
            P(None, "col"),
            P(None, "col"),
            P(),
            P(),
        ),
        out_specs=P("row", "col"),
        check_vma=False,
    )
```

```python
import functools

import jax
import jax.numpy as jnp
from jax import lax
from jax.experimental import pallas as pl
from jax.experimental.pallas import tpu as pltpu
from jax.sharding import PartitionSpec as P

ROOM = 3
MORE = (1, 2, 3, 5)
RING = ((0, 2), (2, 3), (3, 1), (1, 0))
BACK = tuple((to, start) for start, to in RING)

SMEM = pl.BlockSpec(memory_space=pltpu.SMEM)
VMEM = pl.BlockSpec(memory_space=pltpu.VMEM)
ANY = pl.BlockSpec(memory_space=pl.ANY)


def flip(x, axis, size, bit):
    return lax.ppermute(x, axis, [(i, i ^ bit) for i in range(size)])


def places(owners):
    out = []
    for p, owner in enumerate(owners):
        place = jnp.int32(0)
        for before in owners[:p]:
            place = place + (before == owner).astype(jnp.int32)
        out.append((owner, place))
    return out


def panels_of(owners, owner, first, room):
    panel_at = [jnp.int32(0)] * room
    count = jnp.int32(-first)
    for p, other in enumerate(owners):
        for n in range(room):
            panel_at[n] = jnp.where((other == owner) & (count == n), p, panel_at[n])
        count = count + (other == owner).astype(jnp.int32)
    return panel_at, count


def owners_of(owner_ref, shift=0):
    return [owner_ref[p] >> shift for p in range(owner_ref.shape[0])]


def table_of(rowner, lowner, lrank, lscale, rrank, rscale, plan):
    plans = jnp.broadcast_to(plan, rowner.shape)
    return jnp.stack([rowner, lowner, rrank[:, 0], lrank[:, 0], plans]), lscale[:, 0] * rscale[:, 0]


def read_table(table_ref):
    return [[table_ref[n, p] for p in range(table_ref.shape[1])] for n in range(4)]


def call(kernel, name, out, specs, scratch, args, megabytes=1, flops=0, unused=()):
    return pl.pallas_call(
        kernel,
        out_shape=[*out, *unused],
        in_specs=specs,
        out_specs=[VMEM] * len(out) + [ANY] * len(unused),
        scratch_shapes=scratch,
        compiler_params=pltpu.CompilerParams(vmem_limit_bytes=24 << 20),
        cost_estimate=pl.CostEstimate(flops=flops, bytes_accessed=megabytes << 20, transcendentals=0),
        name=name,
    )(*args)


def left_kernel(owner_ref, basis_ref, coef_ref, basis_came, coef_came, out_ref):
    me = lax.axis_index("col")
    room = out_ref.shape[0]
    rows = basis_ref.shape[2]
    panel_at, _ = panels_of(owners_of(owner_ref, 1), me >> 1, 0, 2 * room)
    for n in range(room):
        p = jnp.where((me & 1) == 0, panel_at[n], panel_at[n + room])
        mine = owner_ref[p] == me

        @pl.when(mine)
        def _():
            out_ref[n, :, :rows] = basis_ref[p]
            out_ref[n, :, rows:] = coef_ref[p]

        @pl.when(jnp.logical_not(mine))
        def _():
            out_ref[n, :, :rows] = basis_came[p]
            out_ref[n, :, rows:] = coef_came[p]


def share_left(basis, coef, came, owner):
    panels, rmax, rows = basis.shape
    return call(
        left_kernel,
        "share_left",
        [jax.ShapeDtypeStruct((panels // 2, rmax, rows + coef.shape[2]), basis.dtype)],
        [SMEM] + [VMEM] * 4,
        [],
        (owner, basis, coef, *came),
    )[0]


def spread_left(share, size, after=None):
    mine = [share] + [flip(share, "col", size, bit) for bit in range(2, size, 2)]
    given = list(mine)
    if after is not None:
        given[0], after = lax.optimization_barrier((given[0], after))
    return [*mine, *(flip(x, "col", size, 1) for x in given)], after


def spread_right(x, owner, size):
    me = lax.axis_index("row")
    bit = 1
    while bit < size:
        keep = ((owner & bit) == (me & bit))[:, None, None]
        x = jnp.where(keep, x, flip(x, "row", size, bit))
        bit *= 2
    return x


def pack_kernel(first, owner_ref, coef_ref, basis_ref, out_ref):
    width = coef_ref.shape[2]
    panel_at, _ = panels_of(owners_of(owner_ref), lax.axis_index("row"), first, out_ref.shape[0])
    for n, p in enumerate(panel_at):
        out_ref[n, :, :width] = coef_ref[p]
        out_ref[n, :, width:] = basis_ref[p]


def pack(first, room, owner, coef, basis):
    panels, rmax, width = coef.shape
    return call(
        functools.partial(pack_kernel, first),
        "pack_own_panels",
        [jax.ShapeDtypeStruct((room, rmax, width + basis.shape[2]), coef.dtype)],
        [SMEM, VMEM, VMEM],
        [],
        (owner, coef, basis),
    )[0]


def split(x):
    high = x.astype(jnp.bfloat16)
    return high, (x - high.astype(jnp.float32)).astype(jnp.bfloat16)


def wide_tile(left, coef, lrank, rrank, scale):
    rmax = coef.shape[0]
    rows = left.shape[1] - coef.shape[1]
    core = lax.dot_general(coef, left[:, rows:], (((1,), (1,)), ((), ())), preferred_element_type=jnp.float32)
    at = [lax.broadcasted_iota(jnp.int32, (rmax, rmax), d) for d in range(2)]
    core = jnp.where((at[1] < lrank) & (at[0] < rrank), core * scale, 0.0)
    basis = left[:, :rows]
    high, low = split(core)
    wide = jnp.dot(high, basis, preferred_element_type=jnp.float32)
    return split(wide + jnp.dot(low, basis, preferred_element_type=jnp.float32))


def turned_dot(x, y):
    return lax.dot_general(x, y, (((0,), (0,)), ((), ())), preferred_element_type=jnp.float32)


def near_kernel(first, gathered, chips, unused, table_ref, scale_ref, *refs):
    came, (coef_ref, basis_ref, block_ref), refs = refs[:gathered], refs[gathered : gathered + 3], refs[gathered + 3 :]
    sides, outs, (right, left, flat, high, low, sem) = refs[: 2 * chips], refs[2 * chips : -6], refs[-6:]
    outs = outs[: len(outs) - unused]
    out_ref = outs[0]
    panels, rmax, width = coef_ref.shape
    wide = basis_ref.shape[2]
    me, col = lax.axis_index("row"), lax.axis_index("col")
    per = sides[0].shape[0]
    room = came[0].shape[0] if gathered else 0
    pairs = [(src, left.at[n]) for n, src in enumerate(sides)]
    pairs += [(coef_ref, right.at[pl.ds(0, panels), :, pl.ds(0, width)]), (basis_ref, right.at[pl.ds(0, panels), :, pl.ds(width, wide)])]
    pairs += [(src, right.at[pl.ds(panels + n * room, room)]) for n, src in enumerate(came)]
    pairs += [(block_ref, out_ref)]
    copies = [pltpu.make_async_copy(src, dst, sem.at[n]) for n, (src, dst) in enumerate(pairs)]
    for copy in copies:
        copy.start()
    near = jnp.where((me == 0) | (me == 3), 1, 2)
    owners, lowners, rranks, lranks = read_table(table_ref)
    lefts = []
    for chip, place in places([owner >> 1 for owner in lowners]):
        core = (place // per != (col & 1)).astype(jnp.int32)
        lefts.append(((chip ^ (col >> 1)) + chips * core, lax.rem(place, per)))
    for copy in copies[:-1]:
        copy.wait()
    for p, (owner, place) in enumerate(places(owners)):
        if gathered:
            apart = owner ^ me
            source = jnp.where(apart == near, 0, jnp.where(apart == 3, 2, 1))
            here = (apart != 0) & (source < gathered) & (place >= first) & (place < first + room)
            at = jnp.where(here, panels + source * room + place - first, p)
            rrank_p = jnp.where(here | ((apart == 0) & (first == 0)), rranks[p], 0)
        else:
            at, rrank_p = p, rranks[p]
        tile = right[at]
        columns = pl.ds(p * rmax, rmax)
        high[columns], low[columns] = wide_tile(left[lefts[p]], tile[:, :width], lranks[p], rrank_p, scale_ref[p])
        flat[columns] = tile[:, width:]
    update = turned_dot(high[...], flat[...]) + turned_dot(low[...], flat[...])
    copies[-1].wait()
    out_ref[...] = out_ref[...] - update
    if len(outs) > 1:
        wanted = panels_of(owners, 3 - me, 0, room)[0]
        for apart in (near, 3 - near, 3):
            wanted += panels_of(owners, me ^ apart, room, 1)[0]
        for n, p in enumerate(wanted):
            buffer, at = jnp.int32(0), jnp.int32(0)
            for q in range(panels):
                buffer = jnp.where(p == q, lefts[q][0], buffer)
                at = jnp.where(p == q, lefts[q][1], at)
            outs[1][n] = left[buffer, at]


def far_kernel(table_ref, scale_ref, far_ref, left_ref, block_ref, *refs):
    *more, out_ref, right, high, low, sem = refs
    room, rmax, full = far_ref.shape
    width = full - block_ref.shape[1]
    me = lax.axis_index("row")
    near = jnp.where((me == 0) | (me == 3), 1, 2)
    owners = read_table(table_ref)[0]
    crowded = table_ref[4, 0] == 1
    extra = [pltpu.make_async_copy(src, right.at[pl.ds(n, 1)], sem.at[n]) for n, src in enumerate(more)]

    @pl.when(crowded)
    def _():
        for copy in extra:
            copy.start()

    def apply(first, panel_at, held, tiles):
        for n, p in enumerate(panel_at):
            rrank = jnp.where(held[n], table_ref[2, p], 0)
            columns = pl.ds((first + n) * rmax, rmax)
            high[columns], low[columns] = wide_tile(left_ref[first + n], tiles[n, :, :width], table_ref[3, p], rrank, scale_ref[p])
        columns = pl.ds(first * rmax, len(panel_at) * rmax)
        flat = tiles[:, :, width:].reshape(-1, full - width)
        return turned_dot(high[columns], flat) + turned_dot(low[columns], flat)

    def opposite():
        panel_at, count = panels_of(owners, 3 - me, 0, room)
        return apply(0, panel_at, [n < count for n in range(room)], far_ref)

    @pl.when(jnp.logical_not(crowded))
    def _():
        out_ref[...] = block_ref[...] - opposite()

    @pl.when(crowded)
    def _():
        update = opposite()
        places_at = [panels_of(owners, me ^ apart, room, 1) for apart in (near, 3 - near, 3)]
        panel_at = [at[0] for at, _ in places_at]
        for copy in extra:
            copy.wait()
        update = update + apply(room, panel_at, [count > 0 for _, count in places_at], right)
        out_ref[...] = block_ref[...] - update


def apply_near(first, came, table, coef, basis, sides, block, unused=()):
    panels, rmax, width = coef.shape
    rows, wide = block.shape
    kind = coef.dtype
    room = came[0].shape[0] if came else 0
    out = [jax.ShapeDtypeStruct(block.shape, block.dtype)]
    if len(came) == 2:
        out.append(jax.ShapeDtypeStruct((room + 3, *sides[0].shape[1:]), kind))
    return call(
        functools.partial(near_kernel, first, len(came), len(sides) // 2, len(unused)),
        "apply_near",
        out,
        [SMEM] * 2 + [ANY] * (len(came) + 3 + len(sides)),
        [
            pltpu.VMEM((panels + room * len(came), rmax, width + wide), kind),
            pltpu.VMEM((len(sides), *sides[0].shape), kind),
            pltpu.VMEM((panels * rmax, wide), kind),
            pltpu.VMEM((panels * rmax, rows), kind),
            pltpu.VMEM((panels * rmax, rows), kind),
            pltpu.SemaphoreType.DMA((len(sides) + len(came) + 3,)),
        ],
        (*table, *came, coef, basis, block, *sides),
        megabytes=4,
        flops=1 << 29,
        unused=unused,
    )


def apply_far(far, table, left, block, more):
    room, rmax, full = far.shape
    rows = block.shape[0]
    slots = room + len(more)
    return call(
        far_kernel,
        "apply_far",
        [jax.ShapeDtypeStruct(block.shape, block.dtype)],
        [SMEM] * 2 + [VMEM] * 3 + [ANY] * len(more),
        [
            pltpu.VMEM((len(more), rmax, full), far.dtype),
            pltpu.VMEM((slots * rmax, rows), far.dtype),
            pltpu.VMEM((slots * rmax, rows), far.dtype),
            pltpu.SemaphoreType.DMA((len(more),)),
        ],
        (*table, far, left, block, *more),
        megabytes=3,
        flops=1 << 28,
    )[0]


def finish_near(room, block, ring, back, rowner, table, rcoef, rbasis, sides):
    one = jax.ShapeDtypeStruct((1, rcoef.shape[1], rcoef.shape[2] + rbasis.shape[2]), rcoef.dtype)
    if room:
        own = pack(ROOM, room, rowner, rcoef, rbasis)
        near = lax.ppermute(own, "row", RING), lax.ppermute(own, "row", BACK)
    block, lefts, *unused = apply_near(0, (ring, back), table, rcoef, rbasis, sides, block, () if room == 1 else (one,) * 3)
    if not room:
        return block, lefts, tuple(unused)
    ring, block = lax.optimization_barrier((near[0], block))
    more = *near, lax.ppermute(ring, "row", RING)
    if room == 1:
        return block, lefts, more
    return *apply_near(ROOM, more, table, rcoef, rbasis, sides, block), lefts, tuple(unused)


def plan_of(owner):
    row = lax.broadcasted_iota(jnp.int32, (4, owner.shape[0]), 0)
    held = jnp.sum((owner[None, :] == row).astype(jnp.int32), axis=1)
    plan = jnp.zeros(held.shape, jnp.int32)
    for n, room in enumerate((0, *MORE[:-1])):
        plan = jnp.where(held > ROOM + room, n + 1, plan)
    return jnp.max(plan)


def shards(size, block, lbasis, lcoef, rcoef, rbasis, lrank, lscale, rrank, rscale, lowner, rowner):
    lbasis, lcoef, rcoef, rbasis = (x[:, 0] for x in (lbasis, lcoef, rcoef, rbasis))
    plan = plan_of(rowner)
    table = table_of(rowner, lowner, lrank, lscale, rrank, rscale, plan)
    if size[0] != 4:
        lcame = tuple(flip(x, "col", size[1], 1) for x in (lbasis, lcoef))
        rcoef, rbasis = (spread_right(x, rowner, size[0]) for x in (rcoef, rbasis))
        sides, _ = spread_left(share_left(lbasis, lcoef, lcame, lowner), size[1])
        return apply_near(0, (), table, rcoef, rbasis, sides, block)[0]
    own = pack(0, ROOM, rowner, rcoef, rbasis)
    lbasis, lcoef, own = lax.optimization_barrier((lbasis, lcoef, own))
    lcame = tuple(flip(x, "col", size[1], 1) for x in (lbasis, lcoef))
    ring = lax.ppermute(own, "row", RING)
    share = share_left(lbasis, lcoef, lcame, lowner)
    share, own = lax.optimization_barrier((share, own))
    back = lax.ppermute(own, "row", BACK)
    ring, table, plan = lax.optimization_barrier((ring, table, plan))
    far = lax.ppermute(ring, "row", RING)
    sides, back = spread_left(share, size[1], back)
    plans = [functools.partial(finish_near, room) for room in (0, *MORE)]
    block, lefts, more = lax.switch(plan, plans, block, ring, back, rowner, table, rcoef, rbasis, sides)
    return apply_far(far, table, lefts, block, more)


def solution(mesh):
    size = (mesh.shape["row"], mesh.shape["col"])
    return jax.shard_map(
        functools.partial(shards, size),
        mesh=mesh,
        in_specs=(
            P("row", "col"),
            P(None, "col", None, "row"),
            P(None, "col", None, "row"),
            P(None, "row", None, "col"),
            P(None, "row", None, "col"),
            P(None, "row"),
            P(None, "row"),
            P(None, "col"),
            P(None, "col"),
            P(),
            P(),
        ),
        out_specs=P("row", "col"),
        check_vma=False,
    )
```

```python
import functools

import jax
import jax.numpy as jnp
from jax import lax
from jax.experimental import pallas as pl
from jax.experimental.pallas import tpu as pltpu
from jax.sharding import PartitionSpec as P

ROOM = 3
MORE = (1, 2, 3, 5)
RING = ((0, 2), (2, 3), (3, 1), (1, 0))
BACK = tuple((to, start) for start, to in RING)

SMEM = pl.BlockSpec(memory_space=pltpu.SMEM)
VMEM = pl.BlockSpec(memory_space=pltpu.VMEM)
ANY = pl.BlockSpec(memory_space=pl.ANY)


def flip(x, axis, size, bit):
    return lax.ppermute(x, axis, [(i, i ^ bit) for i in range(size)])


def places(owners):
    out = []
    for p, owner in enumerate(owners):
        place = jnp.int32(0)
        for before in owners[:p]:
            place = place + (before == owner).astype(jnp.int32)
        out.append((owner, place))
    return out


def panels_of(owners, owner, first, room):
    panel_at = [jnp.int32(0)] * room
    count = jnp.int32(-first)
    for p, other in enumerate(owners):
        for n in range(room):
            panel_at[n] = jnp.where((other == owner) & (count == n), p, panel_at[n])
        count = count + (other == owner).astype(jnp.int32)
    return panel_at, count


def owners_of(owner_ref, shift=0):
    return [owner_ref[p] >> shift for p in range(owner_ref.shape[0])]


def table_of(rowner, lowner, lrank, lscale, rrank, rscale, plan):
    plans = jnp.broadcast_to(plan, rowner.shape)
    return jnp.stack([rowner, lowner, rrank[:, 0], lrank[:, 0], plans]), lscale[:, 0] * rscale[:, 0]


def read_table(table_ref):
    return [[table_ref[n, p] for p in range(table_ref.shape[1])] for n in range(4)]


def call(kernel, name, out, specs, scratch, args, megabytes=1, flops=0, unused=()):
    return pl.pallas_call(
        kernel,
        out_shape=[*out, *unused],
        in_specs=specs,
        out_specs=[VMEM] * len(out) + [ANY] * len(unused),
        scratch_shapes=scratch,
        compiler_params=pltpu.CompilerParams(vmem_limit_bytes=24 << 20),
        cost_estimate=pl.CostEstimate(flops=flops, bytes_accessed=megabytes << 20, transcendentals=0),
        name=name,
    )(*args)


def left_kernel(owner_ref, basis_ref, coef_ref, basis_came, coef_came, out_ref):
    me = lax.axis_index("col")
    room = out_ref.shape[0]
    rows = basis_ref.shape[2]
    panel_at, _ = panels_of(owners_of(owner_ref, 1), me >> 1, 0, 2 * room)
    for n in range(room):
        p = jnp.where((me & 1) == 0, panel_at[n], panel_at[n + room])
        mine = owner_ref[p] == me

        @pl.when(mine)
        def _():
            out_ref[n, :, :rows] = basis_ref[p]
            out_ref[n, :, rows:] = coef_ref[p]

        @pl.when(jnp.logical_not(mine))
        def _():
            out_ref[n, :, :rows] = basis_came[p]
            out_ref[n, :, rows:] = coef_came[p]


def share_left(basis, coef, came, owner):
    panels, rmax, rows = basis.shape
    return call(
        left_kernel,
        "share_left",
        [jax.ShapeDtypeStruct((panels // 2, rmax, rows + coef.shape[2]), basis.dtype)],
        [SMEM] + [VMEM] * 4,
        [],
        (owner, basis, coef, *came),
    )[0]


def spread_left(share, size, after=None):
    mine = [share] + [flip(share, "col", size, bit) for bit in range(2, size, 2)]
    given = list(mine)
    if after is not None:
        given[1], after = lax.optimization_barrier((given[1], after))
    return [*mine, *(flip(x, "col", size, 1) for x in given)], after


def spread_right(x, owner, size):
    me = lax.axis_index("row")
    bit = 1
    while bit < size:
        keep = ((owner & bit) == (me & bit))[:, None, None]
        x = jnp.where(keep, x, flip(x, "row", size, bit))
        bit *= 2
    return x


def pack_kernel(first, owner_ref, coef_ref, basis_ref, out_ref):
    width = coef_ref.shape[2]
    panel_at, _ = panels_of(owners_of(owner_ref), lax.axis_index("row"), first, out_ref.shape[0])
    for n, p in enumerate(panel_at):
        out_ref[n, :, :width] = coef_ref[p]
        out_ref[n, :, width:] = basis_ref[p]


def pack(first, room, owner, coef, basis):
    panels, rmax, width = coef.shape
    return call(
        functools.partial(pack_kernel, first),
        "pack_own_panels",
        [jax.ShapeDtypeStruct((room, rmax, width + basis.shape[2]), coef.dtype)],
        [SMEM, VMEM, VMEM],
        [],
        (owner, coef, basis),
    )[0]


def split(x):
    high = x.astype(jnp.bfloat16)
    return high, (x - high.astype(jnp.float32)).astype(jnp.bfloat16)


def wide_tile(left, coef, lrank, rrank, scale):
    rmax = coef.shape[0]
    rows = left.shape[1] - coef.shape[1]
    core = lax.dot_general(coef, left[:, rows:], (((1,), (1,)), ((), ())), preferred_element_type=jnp.float32)
    at = [lax.broadcasted_iota(jnp.int32, (rmax, rmax), d) for d in range(2)]
    core = jnp.where((at[1] < lrank) & (at[0] < rrank), core * scale, 0.0)
    basis = left[:, :rows]
    high, low = split(core)
    wide = jnp.dot(high, basis, preferred_element_type=jnp.float32)
    return split(wide + jnp.dot(low, basis, preferred_element_type=jnp.float32))


def turned_dot(x, y):
    return lax.dot_general(x, y, (((0,), (0,)), ((), ())), preferred_element_type=jnp.float32)


def near_kernel(first, gathered, chips, unused, table_ref, scale_ref, *refs):
    came, (coef_ref, basis_ref, block_ref), refs = refs[:gathered], refs[gathered : gathered + 3], refs[gathered + 3 :]
    sides, outs, (right, left, flat, high, low, sem) = refs[: 2 * chips], refs[2 * chips : -6], refs[-6:]
    outs = outs[: len(outs) - unused]
    out_ref = outs[0]
    panels, rmax, width = coef_ref.shape
    wide = basis_ref.shape[2]
    me, col = lax.axis_index("row"), lax.axis_index("col")
    per = sides[0].shape[0]
    room = came[0].shape[0] if gathered else 0
    pairs = [(src, left.at[n]) for n, src in enumerate(sides)]
    pairs += [(coef_ref, right.at[pl.ds(0, panels), :, pl.ds(0, width)]), (basis_ref, right.at[pl.ds(0, panels), :, pl.ds(width, wide)])]
    pairs += [(src, right.at[pl.ds(panels + n * room, room)]) for n, src in enumerate(came)]
    pairs += [(block_ref, out_ref)]
    copies = [pltpu.make_async_copy(src, dst, sem.at[n]) for n, (src, dst) in enumerate(pairs)]
    for copy in copies:
        copy.start()
    near = jnp.where((me == 0) | (me == 3), 1, 2)
    owners, lowners, rranks, lranks = read_table(table_ref)
    lefts = []
    for chip, place in places([owner >> 1 for owner in lowners]):
        core = (place // per != (col & 1)).astype(jnp.int32)
        lefts.append(((chip ^ (col >> 1)) + chips * core, lax.rem(place, per)))
    for copy in copies[:-1]:
        copy.wait()
    for p, (owner, place) in enumerate(places(owners)):
        if gathered:
            apart = owner ^ me
            source = jnp.where(apart == near, 0, jnp.where(apart == 3, 2, 1))
            here = (apart != 0) & (source < gathered) & (place >= first) & (place < first + room)
            at = jnp.where(here, panels + source * room + place - first, p)
            rrank_p = jnp.where(here | ((apart == 0) & (first == 0)), rranks[p], 0)
        else:
            at, rrank_p = p, rranks[p]
        tile = right[at]
        columns = pl.ds(p * rmax, rmax)
        high[columns], low[columns] = wide_tile(left[lefts[p]], tile[:, :width], lranks[p], rrank_p, scale_ref[p])
        flat[columns] = tile[:, width:]
    update = turned_dot(high[...], flat[...]) + turned_dot(low[...], flat[...])
    copies[-1].wait()
    out_ref[...] = out_ref[...] - update
    if len(outs) > 1:
        wanted = panels_of(owners, 3 - me, 0, room)[0]
        for apart in (near, 3 - near, 3):
            wanted += panels_of(owners, me ^ apart, room, 1)[0]
        for n, p in enumerate(wanted):
            buffer, at = jnp.int32(0), jnp.int32(0)
            for q in range(panels):
                buffer = jnp.where(p == q, lefts[q][0], buffer)
                at = jnp.where(p == q, lefts[q][1], at)
            outs[1][n] = left[buffer, at]


def far_kernel(table_ref, scale_ref, far_ref, left_ref, block_ref, *refs):
    *more, out_ref, right, high, low, sem = refs
    room, rmax, full = far_ref.shape
    width = full - block_ref.shape[1]
    me = lax.axis_index("row")
    near = jnp.where((me == 0) | (me == 3), 1, 2)
    owners = read_table(table_ref)[0]
    crowded = table_ref[4, 0] == 1
    extra = [pltpu.make_async_copy(src, right.at[pl.ds(n, 1)], sem.at[n]) for n, src in enumerate(more)]

    @pl.when(crowded)
    def _():
        for copy in extra:
            copy.start()

    def apply(first, panel_at, held, tiles):
        for n, p in enumerate(panel_at):
            rrank = jnp.where(held[n], table_ref[2, p], 0)
            columns = pl.ds((first + n) * rmax, rmax)
            high[columns], low[columns] = wide_tile(left_ref[first + n], tiles[n, :, :width], table_ref[3, p], rrank, scale_ref[p])
        columns = pl.ds(first * rmax, len(panel_at) * rmax)
        flat = tiles[:, :, width:].reshape(-1, full - width)
        return turned_dot(high[columns], flat) + turned_dot(low[columns], flat)

    def opposite():
        panel_at, count = panels_of(owners, 3 - me, 0, room)
        return apply(0, panel_at, [n < count for n in range(room)], far_ref)

    @pl.when(jnp.logical_not(crowded))
    def _():
        out_ref[...] = block_ref[...] - opposite()

    @pl.when(crowded)
    def _():
        update = opposite()
        places_at = [panels_of(owners, me ^ apart, room, 1) for apart in (near, 3 - near, 3)]
        panel_at = [at[0] for at, _ in places_at]
        for copy in extra:
            copy.wait()
        update = update + apply(room, panel_at, [count > 0 for _, count in places_at], right)
        out_ref[...] = block_ref[...] - update


def apply_near(first, came, table, coef, basis, sides, block, unused=()):
    panels, rmax, width = coef.shape
    rows, wide = block.shape
    kind = coef.dtype
    room = came[0].shape[0] if came else 0
    out = [jax.ShapeDtypeStruct(block.shape, block.dtype)]
    if len(came) == 2:
        out.append(jax.ShapeDtypeStruct((room + 3, *sides[0].shape[1:]), kind))
    return call(
        functools.partial(near_kernel, first, len(came), len(sides) // 2, len(unused)),
        "apply_near",
        out,
        [SMEM] * 2 + [ANY] * (len(came) + 3 + len(sides)),
        [
            pltpu.VMEM((panels + room * len(came), rmax, width + wide), kind),
            pltpu.VMEM((len(sides), *sides[0].shape), kind),
            pltpu.VMEM((panels * rmax, wide), kind),
            pltpu.VMEM((panels * rmax, rows), kind),
            pltpu.VMEM((panels * rmax, rows), kind),
            pltpu.SemaphoreType.DMA((len(sides) + len(came) + 3,)),
        ],
        (*table, *came, coef, basis, block, *sides),
        megabytes=4,
        flops=1 << 29,
        unused=unused,
    )


def apply_far(far, table, left, block, more):
    room, rmax, full = far.shape
    rows = block.shape[0]
    slots = room + len(more)
    return call(
        far_kernel,
        "apply_far",
        [jax.ShapeDtypeStruct(block.shape, block.dtype)],
        [SMEM] * 2 + [VMEM] * 3 + [ANY] * len(more),
        [
            pltpu.VMEM((len(more), rmax, full), far.dtype),
            pltpu.VMEM((slots * rmax, rows), far.dtype),
            pltpu.VMEM((slots * rmax, rows), far.dtype),
            pltpu.SemaphoreType.DMA((len(more),)),
        ],
        (*table, far, left, block, *more),
        megabytes=3,
        flops=1 << 28,
    )[0]


def finish_near(room, block, ring, back, rowner, table, rcoef, rbasis, sides):
    one = jax.ShapeDtypeStruct((1, rcoef.shape[1], rcoef.shape[2] + rbasis.shape[2]), rcoef.dtype)
    if room:
        own = pack(ROOM, room, rowner, rcoef, rbasis)
        near = lax.ppermute(own, "row", RING), lax.ppermute(own, "row", BACK)
    block, lefts, *unused = apply_near(0, (ring, back), table, rcoef, rbasis, sides, block, () if room == 1 else (one,) * 3)
    if not room:
        return block, lefts, tuple(unused)
    ring, block = lax.optimization_barrier((near[0], block))
    more = *near, lax.ppermute(ring, "row", RING)
    if room == 1:
        return block, lefts, more
    return *apply_near(ROOM, more, table, rcoef, rbasis, sides, block), lefts, tuple(unused)


def plan_of(owner):
    row = lax.broadcasted_iota(jnp.int32, (4, owner.shape[0]), 0)
    held = jnp.sum((owner[None, :] == row).astype(jnp.int32), axis=1)
    plan = jnp.zeros(held.shape, jnp.int32)
    for n, room in enumerate((0, *MORE[:-1])):
        plan = jnp.where(held > ROOM + room, n + 1, plan)
    return jnp.max(plan)


def shards(size, block, lbasis, lcoef, rcoef, rbasis, lrank, lscale, rrank, rscale, lowner, rowner):
    lbasis, lcoef, rcoef, rbasis = (x[:, 0] for x in (lbasis, lcoef, rcoef, rbasis))
    plan = plan_of(rowner)
    table = table_of(rowner, lowner, lrank, lscale, rrank, rscale, plan)
    if size[0] != 4:
        lcame = tuple(flip(x, "col", size[1], 1) for x in (lbasis, lcoef))
        rcoef, rbasis = (spread_right(x, rowner, size[0]) for x in (rcoef, rbasis))
        sides, _ = spread_left(share_left(lbasis, lcoef, lcame, lowner), size[1])
        return apply_near(0, (), table, rcoef, rbasis, sides, block)[0]
    own = pack(0, ROOM, rowner, rcoef, rbasis)
    lbasis, lcoef, own = lax.optimization_barrier((lbasis, lcoef, own))
    lcame = tuple(flip(x, "col", size[1], 1) for x in (lbasis, lcoef))
    ring = lax.ppermute(own, "row", RING)
    share = share_left(lbasis, lcoef, lcame, lowner)
    share, own = lax.optimization_barrier((share, own))
    back = lax.ppermute(own, "row", BACK)
    ring, table, plan = lax.optimization_barrier((ring, table, plan))
    far = lax.ppermute(ring, "row", RING)
    sides, back = spread_left(share, size[1], back)
    plans = [functools.partial(finish_near, room) for room in (0, *MORE)]
    block, lefts, more = lax.switch(plan, plans, block, ring, back, rowner, table, rcoef, rbasis, sides)
    return apply_far(far, table, lefts, block, more)


def solution(mesh):
    size = (mesh.shape["row"], mesh.shape["col"])
    return jax.shard_map(
        functools.partial(shards, size),
        mesh=mesh,
        in_specs=(
            P("row", "col"),
            P(None, "col", None, "row"),
            P(None, "col", None, "row"),
            P(None, "row", None, "col"),
            P(None, "row", None, "col"),
            P(None, "row"),
            P(None, "row"),
            P(None, "col"),
            P(None, "col"),
            P(),
            P(),
        ),
        out_specs=P("row", "col"),
        check_vma=False,
    )
```

```python
import functools

import jax
import jax.numpy as jnp
from jax import lax
from jax.experimental import pallas as pl
from jax.experimental.pallas import tpu as pltpu
from jax.sharding import PartitionSpec as P

ROOM = 3
MORE = (1, 2, 5)
RING = ((0, 2), (2, 3), (3, 1), (1, 0))
BACK = tuple((to, start) for start, to in RING)

SMEM = pl.BlockSpec(memory_space=pltpu.SMEM)
VMEM = pl.BlockSpec(memory_space=pltpu.VMEM)
ANY = pl.BlockSpec(memory_space=pl.ANY)


def flip(x, axis, size, bit):
    return lax.ppermute(x, axis, [(i, i ^ bit) for i in range(size)])


def places(owners):
    out = []
    for p, owner in enumerate(owners):
        place = jnp.int32(0)
        for before in owners[:p]:
            place = place + (before == owner).astype(jnp.int32)
        out.append((owner, place))
    return out


def panels_of(owners, owner, first, room):
    panel_at = [jnp.int32(0)] * room
    count = jnp.int32(-first)
    for p, other in enumerate(owners):
        for n in range(room):
            panel_at[n] = jnp.where((other == owner) & (count == n), p, panel_at[n])
        count = count + (other == owner).astype(jnp.int32)
    return panel_at, count


def owners_of(owner_ref, shift=0):
    return [owner_ref[p] >> shift for p in range(owner_ref.shape[0])]


def table_of(rowner, lowner, lrank, lscale, rrank, rscale, plan):
    plans = jnp.broadcast_to(plan, rowner.shape)
    return jnp.stack([rowner, lowner, rrank[:, 0], lrank[:, 0], plans]), lscale[:, 0] * rscale[:, 0]


def read_table(table_ref):
    return [[table_ref[n, p] for p in range(table_ref.shape[1])] for n in range(4)]


def call(kernel, name, out, specs, scratch, args, megabytes=1, flops=0, unused=()):
    return pl.pallas_call(
        kernel,
        out_shape=[*out, *unused],
        in_specs=specs,
        out_specs=[VMEM] * len(out) + [ANY] * len(unused),
        scratch_shapes=scratch,
        compiler_params=pltpu.CompilerParams(vmem_limit_bytes=24 << 20),
        cost_estimate=pl.CostEstimate(flops=flops, bytes_accessed=megabytes << 20, transcendentals=0),
        name=name,
    )(*args)


def left_kernel(owner_ref, basis_ref, coef_ref, basis_came, coef_came, out_ref):
    me = lax.axis_index("col")
    room = out_ref.shape[0]
    rows = basis_ref.shape[2]
    panel_at, _ = panels_of(owners_of(owner_ref, 1), me >> 1, 0, 2 * room)
    for n in range(room):
        p = jnp.where((me & 1) == 0, panel_at[n], panel_at[n + room])
        mine = owner_ref[p] == me

        @pl.when(mine)
        def _():
            out_ref[n, :, :rows] = basis_ref[p]
            out_ref[n, :, rows:] = coef_ref[p]

        @pl.when(jnp.logical_not(mine))
        def _():
            out_ref[n, :, :rows] = basis_came[p]
            out_ref[n, :, rows:] = coef_came[p]


def share_left(basis, coef, came, owner):
    panels, rmax, rows = basis.shape
    return call(
        left_kernel,
        "share_left",
        [jax.ShapeDtypeStruct((panels // 2, rmax, rows + coef.shape[2]), basis.dtype)],
        [SMEM] + [VMEM] * 4,
        [],
        (owner, basis, coef, *came),
    )[0]


def spread_left(share, size, after=None):
    mine = [share] + [flip(share, "col", size, bit) for bit in range(2, size, 2)]
    given = list(mine)
    if after is not None:
        given[2], after = lax.optimization_barrier((given[2], after))
    return [*mine, *(flip(x, "col", size, 1) for x in given)], after


def spread_right(x, owner, size):
    me = lax.axis_index("row")
    bit = 1
    while bit < size:
        keep = ((owner & bit) == (me & bit))[:, None, None]
        x = jnp.where(keep, x, flip(x, "row", size, bit))
        bit *= 2
    return x


def pack_kernel(first, owner_ref, coef_ref, basis_ref, out_ref):
    width = coef_ref.shape[2]
    panel_at, _ = panels_of(owners_of(owner_ref), lax.axis_index("row"), first, out_ref.shape[0])
    for n, p in enumerate(panel_at):
        out_ref[n, :, :width] = coef_ref[p]
        out_ref[n, :, width:] = basis_ref[p]


def pack(first, room, owner, coef, basis):
    panels, rmax, width = coef.shape
    return call(
        functools.partial(pack_kernel, first),
        "pack_own_panels",
        [jax.ShapeDtypeStruct((room, rmax, width + basis.shape[2]), coef.dtype)],
        [SMEM, VMEM, VMEM],
        [],
        (owner, coef, basis),
    )[0]


def split(x):
    high = x.astype(jnp.bfloat16)
    return high, (x - high.astype(jnp.float32)).astype(jnp.bfloat16)


def wide_tile(left, coef, lrank, rrank, scale):
    rmax = coef.shape[0]
    rows = left.shape[1] - coef.shape[1]
    core = lax.dot_general(coef, left[:, rows:], (((1,), (1,)), ((), ())), preferred_element_type=jnp.float32)
    at = [lax.broadcasted_iota(jnp.int32, (rmax, rmax), d) for d in range(2)]
    core = jnp.where((at[1] < lrank) & (at[0] < rrank), core * scale, 0.0)
    basis = left[:, :rows]
    high, low = split(core)
    wide = jnp.dot(high, basis, preferred_element_type=jnp.float32)
    return split(wide + jnp.dot(low, basis, preferred_element_type=jnp.float32))


def turned_dot(x, y):
    return lax.dot_general(x, y, (((0,), (0,)), ((), ())), preferred_element_type=jnp.float32)


def near_kernel(first, gathered, chips, unused, table_ref, scale_ref, *refs):
    came, (coef_ref, basis_ref, block_ref), refs = refs[:gathered], refs[gathered : gathered + 3], refs[gathered + 3 :]
    sides, outs, (right, left, flat, high, low, sem) = refs[: 2 * chips], refs[2 * chips : -6], refs[-6:]
    outs = outs[: len(outs) - unused]
    out_ref = outs[0]
    panels, rmax, width = coef_ref.shape
    wide = basis_ref.shape[2]
    me, col = lax.axis_index("row"), lax.axis_index("col")
    per = sides[0].shape[0]
    room = came[0].shape[0] if gathered else 0
    pairs = [(src, left.at[n]) for n, src in enumerate(sides)]
    pairs += [(coef_ref, right.at[pl.ds(0, panels), :, pl.ds(0, width)]), (basis_ref, right.at[pl.ds(0, panels), :, pl.ds(width, wide)])]
    pairs += [(src, right.at[pl.ds(panels + n * room, room)]) for n, src in enumerate(came)]
    pairs += [(block_ref, out_ref)]
    copies = [pltpu.make_async_copy(src, dst, sem.at[n]) for n, (src, dst) in enumerate(pairs)]
    for copy in copies:
        copy.start()
    near = jnp.where((me == 0) | (me == 3), 1, 2)
    owners, lowners, rranks, lranks = read_table(table_ref)
    lefts = []
    for chip, place in places([owner >> 1 for owner in lowners]):
        core = (place // per != (col & 1)).astype(jnp.int32)
        lefts.append(((chip ^ (col >> 1)) + chips * core, lax.rem(place, per)))
    for copy in copies[:-1]:
        copy.wait()
    for p, (owner, place) in enumerate(places(owners)):
        if gathered:
            apart = owner ^ me
            source = jnp.where(apart == near, 0, jnp.where(apart == 3, 2, 1))
            here = (apart != 0) & (source < gathered) & (place >= first) & (place < first + room)
            at = jnp.where(here, panels + source * room + place - first, p)
            rrank_p = jnp.where(here | ((apart == 0) & (first == 0)), rranks[p], 0)
        else:
            at, rrank_p = p, rranks[p]
        tile = right[at]
        columns = pl.ds(p * rmax, rmax)
        high[columns], low[columns] = wide_tile(left[lefts[p]], tile[:, :width], lranks[p], rrank_p, scale_ref[p])
        flat[columns] = tile[:, width:]
    update = turned_dot(high[...], flat[...]) + turned_dot(low[...], flat[...])
    copies[-1].wait()
    out_ref[...] = out_ref[...] - update
    if len(outs) > 1:
        wanted = panels_of(owners, 3 - me, 0, room)[0]
        for apart in (near, 3 - near, 3):
            wanted += panels_of(owners, me ^ apart, room, 1)[0]
        for n, p in enumerate(wanted):
            buffer, at = jnp.int32(0), jnp.int32(0)
            for q in range(panels):
                buffer = jnp.where(p == q, lefts[q][0], buffer)
                at = jnp.where(p == q, lefts[q][1], at)
            outs[1][n] = left[buffer, at]


def far_kernel(table_ref, scale_ref, far_ref, left_ref, block_ref, *refs):
    *more, out_ref, right, high, low, sem = refs
    room, rmax, full = far_ref.shape
    width = full - block_ref.shape[1]
    me = lax.axis_index("row")
    near = jnp.where((me == 0) | (me == 3), 1, 2)
    owners = read_table(table_ref)[0]
    crowded = table_ref[4, 0] == 1
    extra = [pltpu.make_async_copy(src, right.at[pl.ds(n, 1)], sem.at[n]) for n, src in enumerate(more)]

    @pl.when(crowded)
    def _():
        for copy in extra:
            copy.start()

    def apply(first, panel_at, held, tiles):
        for n, p in enumerate(panel_at):
            rrank = jnp.where(held[n], table_ref[2, p], 0)
            columns = pl.ds((first + n) * rmax, rmax)
            high[columns], low[columns] = wide_tile(left_ref[first + n], tiles[n, :, :width], table_ref[3, p], rrank, scale_ref[p])
        columns = pl.ds(first * rmax, len(panel_at) * rmax)
        flat = tiles[:, :, width:].reshape(-1, full - width)
        return turned_dot(high[columns], flat) + turned_dot(low[columns], flat)

    def opposite():
        panel_at, count = panels_of(owners, 3 - me, 0, room)
        return apply(0, panel_at, [n < count for n in range(room)], far_ref)

    @pl.when(jnp.logical_not(crowded))
    def _():
        out_ref[...] = block_ref[...] - opposite()

    @pl.when(crowded)
    def _():
        update = opposite()
        places_at = [panels_of(owners, me ^ apart, room, 1) for apart in (near, 3 - near, 3)]
        panel_at = [at[0] for at, _ in places_at]
        for copy in extra:
            copy.wait()
        update = update + apply(room, panel_at, [count > 0 for _, count in places_at], right)
        out_ref[...] = block_ref[...] - update


def apply_near(first, came, table, coef, basis, sides, block, unused=()):
    panels, rmax, width = coef.shape
    rows, wide = block.shape
    kind = coef.dtype
    room = came[0].shape[0] if came else 0
    out = [jax.ShapeDtypeStruct(block.shape, block.dtype)]
    if len(came) == 2:
        out.append(jax.ShapeDtypeStruct((room + 3, *sides[0].shape[1:]), kind))
    return call(
        functools.partial(near_kernel, first, len(came), len(sides) // 2, len(unused)),
        "apply_near",
        out,
        [SMEM] * 2 + [ANY] * (len(came) + 3 + len(sides)),
        [
            pltpu.VMEM((panels + room * len(came), rmax, width + wide), kind),
            pltpu.VMEM((len(sides), *sides[0].shape), kind),
            pltpu.VMEM((panels * rmax, wide), kind),
            pltpu.VMEM((panels * rmax, rows), kind),
            pltpu.VMEM((panels * rmax, rows), kind),
            pltpu.SemaphoreType.DMA((len(sides) + len(came) + 3,)),
        ],
        (*table, *came, coef, basis, block, *sides),
        megabytes=4,
        flops=1 << 29,
        unused=unused,
    )


def apply_far(far, table, left, block, more):
    room, rmax, full = far.shape
    rows = block.shape[0]
    slots = room + len(more)
    return call(
        far_kernel,
        "apply_far",
        [jax.ShapeDtypeStruct(block.shape, block.dtype)],
        [SMEM] * 2 + [VMEM] * 3 + [ANY] * len(more),
        [
            pltpu.VMEM((len(more), rmax, full), far.dtype),
            pltpu.VMEM((slots * rmax, rows), far.dtype),
            pltpu.VMEM((slots * rmax, rows), far.dtype),
            pltpu.SemaphoreType.DMA((len(more),)),
        ],
        (*table, far, left, block, *more),
        megabytes=3,
        flops=1 << 28,
    )[0]


def finish_near(room, block, ring, back, rowner, table, rcoef, rbasis, sides):
    one = jax.ShapeDtypeStruct((1, rcoef.shape[1], rcoef.shape[2] + rbasis.shape[2]), rcoef.dtype)
    if room:
        own = pack(ROOM, room, rowner, rcoef, rbasis)
        near = lax.ppermute(own, "row", RING), lax.ppermute(own, "row", BACK)
    block, lefts, *unused = apply_near(0, (ring, back), table, rcoef, rbasis, sides, block, () if room == 1 else (one,) * 3)
    if not room:
        return block, lefts, tuple(unused)
    ring, block = lax.optimization_barrier((near[0], block))
    more = *near, lax.ppermute(ring, "row", RING)
    if room == 1:
        return block, lefts, more
    return *apply_near(ROOM, more, table, rcoef, rbasis, sides, block), lefts, tuple(unused)


def plan_of(owner):
    row = lax.broadcasted_iota(jnp.int32, (4, owner.shape[0]), 0)
    held = jnp.sum((owner[None, :] == row).astype(jnp.int32), axis=1)
    plan = jnp.zeros(held.shape, jnp.int32)
    for n, room in enumerate((0, *MORE[:-1])):
        plan = jnp.where(held > ROOM + room, n + 1, plan)
    return jnp.max(plan)


def shards(size, block, lbasis, lcoef, rcoef, rbasis, lrank, lscale, rrank, rscale, lowner, rowner):
    lbasis, lcoef, rcoef, rbasis = (x[:, 0] for x in (lbasis, lcoef, rcoef, rbasis))
    plan = plan_of(rowner)
    table = table_of(rowner, lowner, lrank, lscale, rrank, rscale, plan)
    if size[0] != 4:
        lcame = tuple(flip(x, "col", size[1], 1) for x in (lbasis, lcoef))
        rcoef, rbasis = (spread_right(x, rowner, size[0]) for x in (rcoef, rbasis))
        sides, _ = spread_left(share_left(lbasis, lcoef, lcame, lowner), size[1])
        return apply_near(0, (), table, rcoef, rbasis, sides, block)[0]
    own = pack(0, ROOM, rowner, rcoef, rbasis)
    lbasis, lcoef, own = lax.optimization_barrier((lbasis, lcoef, own))
    lcame = tuple(flip(x, "col", size[1], 1) for x in (lbasis, lcoef))
    ring = lax.ppermute(own, "row", RING)
    share = share_left(lbasis, lcoef, lcame, lowner)
    share, own = lax.optimization_barrier((share, own))
    back = lax.ppermute(own, "row", BACK)
    ring, table, plan = lax.optimization_barrier((ring, table, plan))
    far = lax.ppermute(ring, "row", RING)
    sides, back = spread_left(share, size[1], back)
    plans = [functools.partial(finish_near, room) for room in (0, *MORE)]
    block, lefts, more = lax.switch(plan, plans, block, ring, back, rowner, table, rcoef, rbasis, sides)
    return apply_far(far, table, lefts, block, more)


def solution(mesh):
    size = (mesh.shape["row"], mesh.shape["col"])
    return jax.shard_map(
        functools.partial(shards, size),
        mesh=mesh,
        in_specs=(
            P("row", "col"),
            P(None, "col", None, "row"),
            P(None, "col", None, "row"),
            P(None, "row", None, "col"),
            P(None, "row", None, "col"),
            P(None, "row"),
            P(None, "row"),
            P(None, "col"),
            P(None, "col"),
            P(),
            P(),
        ),
        out_specs=P("row", "col"),
        check_vma=False,
    )
```
